128 devices in a mesh: grp: 4 (over y_hi, core), blk: 32 (over y_lo, z, x).
Axes of the slice: x: 4, y: 4 (y_hi: 2, y_lo: 2; y = y_hi * 2 + y_lo), z: 4, core: 2. Of those that a mesh axis runs over, the one named last changes fastest.
Arguments:
- embeddings: bfloat16 [49152, 1024], P(('grp', 'blk')), may hold values from -6 to 6
- cluster_id: int32 [49152], P(('grp', 'blk')), may hold values from 0 to 7, as said below
- source_id: int32 [49152], P(('grp', 'blk')), may hold values from 0 to 65535
Outputs:
- max_similarity: float32 [49152], P(('grp', 'blk'))
The draws below stay inside these ranges and needn't reach their ends.
Inputs may be any that keep to these rules, and one draw needn't show every extreme that they name: `cluster_id`: within each group's 12288 rows the ids start at 0 at the group's first row, rise by 0 or 1 from one row to the next, and end at 7.
All inputs are finite; a program needn't handle non-finite values.
Results may differ from the reference program's by a relative error of at most 0.0013.
Values may be sent and summed in bfloat16 or wider, within the bound.
No kernel may reach another device: no remote copies, remote signals or barrier semaphores. Data moves between devices by JAX's collectives and lax.ppermute only.
A program may use at most 64 MiB of HBM per device.

```python
import math
import jax
import jax.numpy as jnp
import numpy as np
from jax import lax

D = 1024
ROWS_DEV = 384
SOURCES = 65536
CLUSTERS = 8
GROUPS = 4
SLAB = 12288
ROWS = 49152
N_GRP = 4
N_BLK = 32


def draw_cluster_id(key, part):
    key = jax.random.fold_in(key, 7)
    first_key, second_key, third_key = jax.random.split(key, 3)
    heavy = jax.random.randint(first_key, (), 0, GROUPS)
    members = jnp.arange(GROUPS, dtype=jnp.int32)
    length = jnp.where(members == heavy, SLAB * 5 // 8, SLAB // 8)
    start = jax.random.randint(second_key, (GROUPS,), 0, 1 << 30) % (SLAB - length + 1)
    position = jnp.arange(SLAB, dtype=jnp.int32)[None, :]
    finish = start[:, None] + length[:, None]
    interior = (position > start[:, None]) & (position < finish)
    forced = ((position == start[:, None]) | (position == finish)) & (position >= 1)
    allowed = (position >= 1) & jnp.logical_not(interior)
    noise = jax.random.randint(third_key, (GROUPS, SLAB), 0, 1024)
    level = jnp.where(forced, 0, jnp.where(allowed, 1 + noise, 4096))
    scores = level * SLAB + position
    cuts = CLUSTERS - 1
    lowest = -lax.top_k(-scores, cuts)[0]
    threshold = lowest[:, cuts - 1]
    begins = (scores <= threshold[:, None]) | (position == 0)
    labels = jnp.cumsum(begins.astype(jnp.int32), axis=1) - 1
    return labels.reshape(GROUPS * SLAB).astype(jnp.int32)


def place_ends(result, rng, low, top_value):
    index_at = [jax.random.randint(jax.random.fold_in(rng, axis), (), 0, length) for axis, length in enumerate(result.shape)]
    widest = result.shape.index(max(result.shape))
    neighbour = index_at[:widest] + [(index_at[widest] + 1) % result.shape[widest]] + index_at[widest + 1:]
    return result.at[tuple(index_at)].set(low).at[tuple(neighbour)].set(top_value)


def level_of(rng, extent, pieces, low, largest):
    level = 1.0
    for axis_at, blocks in pieces:
        heights = jax.random.uniform(jax.random.fold_in(jax.random.fold_in(rng, 6), axis_at), (blocks,), jnp.float32, low / len(pieces), largest / len(pieces))
        level = level * jnp.repeat(jnp.exp(heights), extent[axis_at] // blocks).reshape((-1,) + (1,) * (len(extent) - 1 - axis_at))
    return level


def cumulative_ranks(count, slope):
    loads = [(1 << 20) // math.isqrt(grade ** slope) + 1 for grade in range(1, count + 1)]
    scale = 1 + sum(loads) // (1 << 30)
    return np.cumsum(np.array([max(1, weight // scale) for weight in loads]))


def ranked(key, shape, count, lean):
    table = cumulative_ranks(count, lean)
    lot = jax.random.randint(jax.random.fold_in(key, 1), shape, 0, int(table[count - 1]))
    standing = jnp.searchsorted(jnp.asarray(table, jnp.int32), lot, side="right")
    return jax.random.permutation(jax.random.fold_in(key, 2), count)[standing].astype(jnp.int32)


def scatter_about(stream_key, dims, spread, limit, cuts=(), held_as=jnp.bfloat16):
    values = spread * jax.random.normal(stream_key, dims, jnp.float32)
    if cuts:
        values = values * level_of(stream_key, dims, cuts, -0.22, 0.18)
    return jnp.clip(values, -limit, limit).astype(held_as)


def setup_inputs(seed: int = 0) -> dict:
    splits = jax.random.split(jax.random.key(seed), 4)
    return {
        "embeddings": scatter_about(splits[0], (ROWS, D), 1.0, 6.0, ((0, 128),)),
        "cluster_id": draw_cluster_id(jax.random.fold_in(splits[3], 71), 0),
        "source_id": place_ends(ranked(splits[2], (ROWS,), SOURCES, 2), jax.random.fold_in(splits[2], 3), 0, SOURCES - 1).astype(jnp.int32),
    }


def normalize(embeddings):
    widened = embeddings.astype(jnp.float32)
    factor = lax.rsqrt(lax.optimization_barrier(jnp.mean(widened * widened, axis=1, keepdims=True)) + 1e-06) / math.sqrt(widened.shape[1])
    return (widened * factor).astype(jnp.bfloat16)

def masked_scores(own_rows, own_ids, own_source, far_rows, far_ids, far_source):
    scores = lax.dot_general(own_rows, far_rows, (((1,), (1,)), ((), ())), preferred_element_type=jnp.float32)
    partner = (own_ids[:, None] == far_ids[None, :]) & (own_source[:, None] != far_source[None, :])
    return jnp.where(partner, scores, -1.0)

def intersecting(own_ids, far_ids):
    return (own_ids[0] <= far_ids[-1]) & (far_ids[0] <= own_ids[-1])

def row_maxima(own_block, far_block):
    floor_rows = jnp.full((own_block[0].shape[0],), -1.0, jnp.float32)
    return lax.cond(intersecting(own_block[1], far_block[1]), lambda: lax.optimization_barrier(jnp.max(masked_scores(*own_block, *far_block), axis=1)), lambda: floor_rows)

def reference(embeddings, cluster_id, source_id):
    unit_rows = normalize(embeddings).reshape(N_GRP * N_BLK, ROWS_DEV, D)
    block_ids = cluster_id.reshape(N_GRP * N_BLK, ROWS_DEV)
    block_source = source_id.reshape(N_GRP * N_BLK, ROWS_DEV)

    def one_block(index):
        group_start = index // N_BLK * N_BLK
        own_block = (unit_rows[index], block_ids[index], block_source[index])

        def visit(column, best_rows):
            far_index = (group_start + column).astype(jnp.int32)
            far_block = (unit_rows[far_index], block_ids[far_index], block_source[far_index])
            return jnp.maximum(best_rows, row_maxima(own_block, far_block))
        return lax.fori_loop(0, N_BLK, visit, jnp.full((ROWS_DEV,), -1.0, jnp.float32))
    results = lax.map(one_block, jnp.arange(N_GRP * N_BLK, dtype=jnp.int32))
    return results.reshape(N_GRP * N_BLK * ROWS_DEV)
```

```python
import functools

import jax
import jax.numpy as jnp
import numpy as np
from jax import lax
from jax.experimental import pallas as pl
from jax.experimental.pallas import tpu as pltpu
from jax.sharding import PartitionSpec as P

TORUS = (2, 4, 4)
OFFSETS = ((0, 0, 0), (0, 0, 1), (0, 1, 0), (0, 3, 0), (1, 0, 3), (0, 0, 2), (1, 2, 0), (1, 0, 2))
FIRST = ((1, 0, (0, 0, 1)), (2, 0, (0, 1, 0)), (4, 0, (1, 0, 3)), (3, 0, (0, 3, 0)))
SECOND = ((5, 1, (0, 0, 1)), (6, 2, (1, 1, 0)), (7, 4, (0, 0, 3)))
EARLY = 5
ROWS = 384
TAIL = 16
BLOCK = ROWS + TAIL
WIDTH = 1024
COUNT = len(OFFSETS)


def difference(a, b):
    return tuple((p - q) % n for p, q, n in zip(a, b, TORUS))


def chosen_pairs():
    best = {}
    for q in range(COUNT):
        for p in range(q + 1):
            d = difference(OFFSETS[q], OFFSETS[p])
            key = min(d, difference((0, 0, 0), d))
            if key not in best:
                best[key] = (p, q)
    assert len(best) == 20
    pairs = sorted(best.values(), key=lambda t: (t[1], t[0]))
    return [t for t in pairs if t[1] < EARLY], [t for t in pairs if t[1] >= EARLY]


EARLY_PAIRS, LATE_PAIRS = chosen_pairs()


def flat(y, z, x):
    return ((y % TORUS[0]) * TORUS[1] + z % TORUS[1]) * TORUS[2] + x % TORUS[2]


def receive(array, by, back=False):
    links = []
    for y in range(TORUS[0]):
        for z in range(TORUS[1]):
            for x in range(TORUS[2]):
                far, near = flat(y + by[0], z + by[1], x + by[2]), flat(y, z, x)
                links.append((near, far) if back else (far, near))
    return lax.ppermute(array, "blk", links)


def prepare_kernel(embeddings, cluster, source, out):
    @pl.loop(0, ROWS // 64)
    def _(step):
        rows = pl.ds(pl.multiple_of(step * 64, 64), 64)
        widened = embeddings[rows, :].astype(jnp.float32)
        factor = lax.rsqrt(jnp.mean(widened * widened, axis=1, keepdims=True) + 1e-06) / 32.0
        out[rows, :] = (widened * factor).astype(jnp.bfloat16)

    line = lax.broadcasted_iota(jnp.int32, (TAIL, ROWS), 0)
    ids = source[...]
    tail = jnp.where(line == 0, cluster[...], jnp.where(line == 1, ids // 256, jnp.where(line == 2, ids % 256, 0)))
    out[ROWS:, :ROWS] = tail.astype(jnp.float32).astype(jnp.bfloat16)
    out[ROWS:, ROWS:] = jnp.zeros((TAIL, WIDTH - ROWS), jnp.bfloat16)


def prepare(embeddings, cluster_id, source_id):
    return pl.pallas_call(
        prepare_kernel,
        out_shape=jax.ShapeDtypeStruct((BLOCK, WIDTH), jnp.bfloat16),
        in_specs=[pl.BlockSpec(memory_space=pltpu.VMEM)] * 3,
        out_specs=pl.BlockSpec(memory_space=pltpu.VMEM),
        compiler_params=pltpu.CompilerParams(vmem_limit_bytes=8 << 20),
        name="prepare",
    )(embeddings, cluster_id.reshape(1, ROWS), source_id.reshape(1, ROWS))


def score_kernel(used, pairs, first, *refs):
    n = len(used)
    lefts, rights, blocks = refs[0], refs[1], refs[2 : 2 + n]
    refs = refs[2 + n :]
    if not first:
        earlier, refs = refs[0], refs[1:]
    outs = refs[: 1 if first else COUNT]
    held, words, word_columns, over_lanes, over_rows, sems = refs[len(outs) :]
    copies = [pltpu.make_async_copy(b, held.at[i], sems.at[i]) for i, b in enumerate(blocks)]
    for copy in copies:
        copy.start()
    over_lanes[...] = jnp.full(over_lanes.shape, -1.0, jnp.float32)
    over_rows[...] = jnp.full(over_rows.shape, -1.0, jnp.float32)
    for i, copy in enumerate(copies):
        copy.wait()
        ids = held[i, ROWS:, :ROWS].astype(jnp.float32)
        word = ids[0:1] * 65536.0 + ids[1:2] * 256.0 + ids[2:3]
        words[i] = jnp.broadcast_to(word, (8, ROWS)).astype(jnp.int32)
        word_columns[i] = jnp.broadcast_to(word, (128, ROWS)).T.astype(jnp.int32)

    @pl.loop(0, len(pairs))
    def _(step):
        p, q = lefts[step], rights[step]
        scores = lax.dot_general(
            held[p, :ROWS, :], held[q, :ROWS, :], (((1,), (1,)), ((), ())), preferred_element_type=jnp.float32
        )
        near = word_columns[p]
        far = words[q, 0:1, :]
        best = over_lanes[p]
        down = []
        for k in range(ROWS // 128):
            mixed = near ^ far[:, k * 128 : (k + 1) * 128]
            partner = (mixed > 0) & (mixed < 65536)
            kept = jnp.where(partner, scores[:, k * 128 : (k + 1) * 128], -1.0)
            best = jnp.maximum(best, kept)
            down.append(jnp.max(kept.reshape(ROWS // 8, 8, 128), axis=0))
        over_lanes[p] = best
        over_rows[q] = jnp.maximum(over_rows[q], jnp.concatenate(down, axis=1))

    results = {}
    for i, b in enumerate(used):
        results[b] = jnp.maximum(
            jnp.max(over_lanes[i].T, axis=0, keepdims=True), jnp.max(over_rows[i], axis=0, keepdims=True)
        )
    if first:
        outs[0][...] = jnp.concatenate([results.get(b, jnp.full((1, ROWS), -1.0, jnp.float32)) for b in range(8)], axis=0)
    else:
        for b in range(COUNT):
            value = earlier[b : b + 1, :]
            outs[b][...] = jnp.maximum(value, results[b]) if b in results else value


def score(blocks, pairs, earlier=None):
    first = earlier is None
    used = sorted({b for t in pairs for b in t})
    n = len(used)
    lefts = jnp.asarray([used.index(p) for p, _ in pairs], jnp.int32)
    rights = jnp.asarray([used.index(q) for _, q in pairs], jnp.int32)
    vmem, smem, free = (pl.BlockSpec(memory_space=m) for m in (pltpu.VMEM, pltpu.SMEM, pl.ANY))
    row = jax.ShapeDtypeStruct((1, ROWS), jnp.float32)
    return pl.pallas_call(
        functools.partial(score_kernel, used, pairs, first),
        out_shape=jax.ShapeDtypeStruct((8, ROWS), jnp.float32) if first else [row] * COUNT,
        in_specs=[smem, smem] + [free] * n + ([] if first else [vmem]),
        out_specs=vmem if first else [vmem] * COUNT,
        scratch_shapes=[
            pltpu.VMEM((n, BLOCK, WIDTH), jnp.bfloat16),
            pltpu.VMEM((n, 8, ROWS), jnp.int32),
            pltpu.VMEM((n, ROWS, 128), jnp.int32),
            pltpu.VMEM((n, ROWS, 128), jnp.float32),
            pltpu.VMEM((n, 8, ROWS), jnp.float32),
            pltpu.SemaphoreType.DMA((n,)),
        ],
        compiler_params=pltpu.CompilerParams(vmem_limit_bytes=24 << 20),
        cost_estimate=pl.CostEstimate(
            flops=2 * len(pairs) * ROWS * ROWS * WIDTH, bytes_accessed=n * BLOCK * WIDTH * 2, transcendentals=0
        ),
        name="score_early" if first else "score_late",
    )(lefts, rights, *[blocks[b] for b in used], *([] if first else [earlier]))


def local(embeddings, cluster_id, source_id):
    blocks = {0: prepare(embeddings, cluster_id, source_id)}
    for block, parent, by in FIRST:
        blocks[block] = receive(blocks[parent], by)
    for block, parent, by in SECOND:
        blocks[block] = receive(blocks[parent], by)
    earlier = score(blocks, EARLY_PAIRS)
    best = score(blocks, LATE_PAIRS, earlier)
    own = best[0]
    for b in range(1, COUNT):
        own = jnp.maximum(own, receive(best[b], OFFSETS[b], back=True))
    return own.reshape(ROWS)


def solution(mesh):
    return jax.shard_map(
        local,
        mesh=mesh,
        in_specs=(P(("grp", "blk"), None), P(("grp", "blk")), P(("grp", "blk"))),
        out_specs=P(("grp", "blk")),
        check_vma=False,
    )
```

```python
import functools

import jax
import jax.numpy as jnp
from jax import lax
from jax.experimental import pallas as pl
from jax.experimental.pallas import tpu as pltpu
from jax.sharding import PartitionSpec as P

TORUS = (2, 4, 4)
OFFSETS = (
    (0, 0, 0),
    (0, 0, 1),
    (0, 1, 3),
    (0, 3, 0),
    (1, 0, 0),
    (0, 2, 3),
    (1, 1, 2),
    (0, 0, 2),
    (0, 2, 0),
)
FIRST = ((3, (0, 3, 0)), (1, (0, 0, 1)), (2, (0, 1, 3)), (4, (1, 0, 0)))
SECOND = ((8, 3, (0, 3, 0)), (7, 1, (0, 0, 1)), (6, 2, (1, 0, 3)), (5, 2, (0, 1, 0)))
ROWS = 384
TAIL = 16
BLOCK = ROWS + TAIL
WIDTH = 1024
STEPS = {
    "early": (
        (0, 1, 2, 3, 4),
        (
            (0, 0, 4, (0, 1, 2, 3, 4)),
            (1, 2, 4, (1, 2, 3, 4)),
            (2, 3, 4, (2, 3, 4)),
            (3, 4, 4, (3, 4)),
        ),
        (0, 1, 2, 3, 4),
    ),
    "middle": (
        (1, 4, 6, 5, 3, 0),
        ((5, 0, 2, (5, 4, 6)), (6, 4, 5, (6, 0))),
        (0, 4, 5, 6),
    ),
    "late": (
        (7, 8, 0, 4),
        ((0, 0, 1, (0,)), (4, 0, 1, (4,))),
        (0, 4),
    ),
}


def difference(a, b):
    return tuple((p - q) % n for p, q, n in zip(a, b, TORUS))


def check():
    met = []
    for order, strips, _ in STEPS.values():
        for a, first, last, sides in strips:
            for b in order[first : last + 1]:
                met += [difference(OFFSETS[b], OFFSETS[a])] * (a in sides)
                met += [difference(OFFSETS[a], OFFSETS[b])] * (b in sides and b != a)
    assert len(set(met)) == 32
    for block, by in FIRST:
        assert OFFSETS[block] == by
    for block, parent, by in SECOND:
        assert difference(OFFSETS[block], OFFSETS[parent]) == by


check()


def flat(y, z, x):
    return ((y % TORUS[0]) * TORUS[1] + z % TORUS[1]) * TORUS[2] + x % TORUS[2]


def receive(array, by, back=False):
    links = []
    for y in range(TORUS[0]):
        for z in range(TORUS[1]):
            for x in range(TORUS[2]):
                far, near = flat(y + by[0], z + by[1], x + by[2]), flat(y, z, x)
                links.append((near, far) if back else (far, near))
    return lax.ppermute(array, "blk", links)


def prepare_kernel(embeddings, cluster, source, out):
    @pl.loop(0, ROWS // 64)
    def _(step):
        rows = pl.ds(pl.multiple_of(step * 64, 64), 64)
        widened = embeddings[rows, :].astype(jnp.float32)
        factor = lax.rsqrt(jnp.mean(widened * widened, axis=1, keepdims=True) + 1e-06) / 32.0
        out[rows, :] = (widened * factor).astype(jnp.bfloat16)

    line = lax.broadcasted_iota(jnp.int32, (TAIL, ROWS), 0)
    ids = source[...].reshape(1, ROWS)
    clusters = cluster[...].reshape(1, ROWS)
    tail = jnp.where(line == 0, clusters, jnp.where(line == 1, ids // 256, jnp.where(line == 2, ids % 256, 0)))
    out[ROWS:, :ROWS] = tail.astype(jnp.float32).astype(jnp.bfloat16)
    out[ROWS:, ROWS:] = jnp.zeros((TAIL, WIDTH - ROWS), jnp.bfloat16)


def prepare(embeddings, cluster_id, source_id):
    return pl.pallas_call(
        prepare_kernel,
        out_shape=jax.ShapeDtypeStruct((BLOCK, WIDTH), jnp.bfloat16),
        in_specs=[pl.BlockSpec(memory_space=pltpu.VMEM)] * 3,
        out_specs=pl.BlockSpec(memory_space=pltpu.VMEM),
        compiler_params=pltpu.CompilerParams(vmem_limit_bytes=8 << 20),
        name="prepare",
    )(embeddings, cluster_id, source_id)


def score_kernel(step, given, *refs):
    order, strips, results = STEPS[step]
    n = len(order)
    place = {b: i for i, b in enumerate(order)}
    blocks, refs = refs[:n], refs[n:]
    earlier, refs = dict(zip(given, refs)), refs[len(given) :]
    outs, refs = dict(zip(results, refs)), refs[len(results) :]
    held, ids, sems = refs
    copies = []
    for i, block in enumerate(blocks):
        copies.append(pltpu.make_async_copy(block.at[:ROWS], held.at[pl.ds(i * ROWS, ROWS)], sems.at[0, i]))
        copies.append(pltpu.make_async_copy(block.at[ROWS:], ids.at[i], sems.at[1, i]))
    for copy in copies:
        copy.start()
    for copy in copies:
        copy.wait()

    def word(b):
        parts = ids[place[b], :, :ROWS].astype(jnp.float32)
        return parts[0:1] * 65536.0 + parts[1:2] * 256.0 + parts[2:3]

    def words(b):
        return word(b).astype(jnp.int32)

    def word_columns(b):
        return jnp.broadcast_to(word(b), (128, ROWS)).T.astype(jnp.int32)

    over_lanes, over_rows = {}, {}

    def update(table, b, value):
        table[b] = jnp.maximum(table[b], value) if b in table else value

    for a, first, last, sides in strips:
        scores = lax.dot_general(
            held[place[a] * ROWS : (place[a] + 1) * ROWS, :],
            held[first * ROWS : (last + 1) * ROWS, :],
            (((1,), (1,)), ((), ())),
            preferred_element_type=jnp.float32,
        )
        near = word_columns(a)
        for i in range(first, last + 1):
            b = order[i]
            far = words(b)
            down = []
            for k in range(ROWS // 128):
                at = (i - first) * ROWS + k * 128
                mixed = near ^ far[:, k * 128 : (k + 1) * 128]
                partner = (mixed > 0) & (mixed < 65536)
                kept = jnp.where(partner, scores[:, at : at + 128], -1.0)
                if a in sides:
                    update(over_lanes, a, kept)
                down.append(jnp.max(kept.reshape(ROWS // 8, 8, 128), axis=0))
            if b in sides and b != a:
                update(over_rows, b, jnp.concatenate(down, axis=1))

    for b in results:
        value = jnp.full((1, ROWS), -1.0, jnp.float32)
        if b in over_lanes:
            value = jnp.maximum(value, jnp.max(over_lanes[b].T, axis=0, keepdims=True))
        if b in over_rows:
            value = jnp.maximum(value, jnp.max(over_rows[b], axis=0, keepdims=True))
        if b in earlier:
            value = jnp.maximum(value, earlier[b][...])
        outs[b][...] = value


def score(step, blocks, earlier):
    order, strips, results = STEPS[step]
    n = len(order)
    given = tuple(b for b in results if b in earlier)
    pairs = sum(last + 1 - first for _, first, last, _ in strips)
    vmem = pl.BlockSpec(memory_space=pltpu.VMEM)
    values = pl.pallas_call(
        functools.partial(score_kernel, step, given),
        out_shape=[jax.ShapeDtypeStruct((1, ROWS), jnp.float32)] * len(results),
        in_specs=[pl.BlockSpec(memory_space=pl.ANY)] * n + [vmem] * len(given),
        out_specs=[vmem] * len(results),
        scratch_shapes=[
            pltpu.VMEM((n * ROWS, WIDTH), jnp.bfloat16),
            pltpu.VMEM((n, TAIL, WIDTH), jnp.bfloat16),
            pltpu.SemaphoreType.DMA((2, n)),
        ],
        compiler_params=pltpu.CompilerParams(vmem_limit_bytes=24 << 20),
        cost_estimate=pl.CostEstimate(
            flops=2 * pairs * ROWS * ROWS * WIDTH, bytes_accessed=n * BLOCK * WIDTH * 2, transcendentals=0
        ),
        name="score_" + step,
    )(*[blocks[b] for b in order], *[earlier[b] for b in given])
    return dict(zip(results, values))


def local(embeddings, cluster_id, source_id):
    blocks = {0: prepare(embeddings, cluster_id, source_id)}
    for block, by in FIRST:
        blocks[block] = receive(blocks[0], by)
    for block, parent, by in SECOND:
        blocks[block] = receive(blocks[parent], by)
    early = score("early", blocks, {})
    middle = score("middle", blocks, {b: early[b] for b in (0, 4)})
    late = score("late", blocks, {b: middle[b] for b in (0, 4)})
    own = late[0]
    for b, values in ((1, early), (2, early), (3, early), (5, middle), (6, middle), (4, late)):
        own = jnp.maximum(own, receive(values[b], OFFSETS[b], back=True))
    return own.reshape(ROWS)


def solution(mesh):
    return jax.shard_map(
        local,
        mesh=mesh,
        in_specs=(P(("grp", "blk"), None), P(("grp", "blk")), P(("grp", "blk"))),
        out_specs=P(("grp", "blk")),
        check_vma=False,
    )
```

```python
import functools

import jax
import jax.numpy as jnp
from jax import lax
from jax.experimental import pallas as pl
from jax.experimental.pallas import tpu as pltpu
from jax.sharding import PartitionSpec as P

TORUS = (2, 4, 4)
OFFSETS = (
    (0, 0, 0),
    (0, 0, 3),
    (0, 1, 0),
    (0, 3, 1),
    (1, 0, 0),
    (0, 0, 2),
    (0, 2, 0),
    (0, 2, 2),
    (1, 0, 3),
)
FIRST = ((1, (0, 0, 3)), (2, (0, 1, 0)), (3, (0, 3, 1)), (4, (1, 0, 0)))
SECOND = ((8, 1, (1, 0, 0)), (5, 1, (0, 0, 3)), (6, 2, (0, 1, 0)), (7, 3, (0, 3, 1)))
ROWS = 384
TAIL = 16
BLOCK = ROWS + TAIL
WIDTH = 1024
STRIPE = 64
STRIPES = ROWS // STRIPE
STEPS = {
    "early": (
        (0, 1, 2, 3, 4),
        ((0, 0, 0, 4, (0, 2, 3)), (1, 1, 2, 4, (2, 3, 4)), (2, 2, 3, 4, (2, 3, 4)), (3, 3, 4, 4, (3, 4))),
    ),
    "middle": ((0, 2, 3, 4, 8, 5), ((4, 4, 0, 3, (2, 3, 8)), (5, 5, 0, 3, (0, 2, 3, 4)))),
    "late": ((8, 4, 6, 7), ((0, 1, 2, 3, (4, 8)),)),
    "last": ((0, 6, 7), ((0, 0, 1, 2, (0,)),)),
}


def difference(a, b):
    return tuple((p - q) % n for p, q, n in zip(a, b, TORUS))


def products(step):
    order, strips = STEPS[step]
    for first, last, left, right, sides in strips:
        yield order[first : last + 1], order[left : right + 1], sides


def targets(step):
    return tuple(sorted({b for rows, columns, sides in products(step) for b in sides if b in rows + columns}))


def check():
    met = set()
    for step in STEPS:
        for rows, columns, sides in products(step):
            for a in rows:
                for b in columns:
                    met |= {difference(OFFSETS[b], OFFSETS[a])} if a in sides else set()
                    met |= {difference(OFFSETS[a], OFFSETS[b])} if b in sides else set()
    assert len(met) == 32
    assert all(OFFSETS[block] == by for block, by in FIRST)
    assert all(difference(OFFSETS[block], OFFSETS[parent]) == by for block, parent, by in SECOND)


check()


def flat(y, z, x):
    return ((y % TORUS[0]) * TORUS[1] + z % TORUS[1]) * TORUS[2] + x % TORUS[2]


def receive(array, by, back=False):
    links = []
    for y in range(TORUS[0]):
        for z in range(TORUS[1]):
            for x in range(TORUS[2]):
                far, near = flat(y + by[0], z + by[1], x + by[2]), flat(y, z, x)
                links.append((near, far) if back else (far, near))
    return lax.ppermute(array, "blk", links)


def prepare_kernel(embeddings, cluster, source, out, raw, clusters, sources, unit, sems):
    def copy(source_rows, target_rows, sem):
        return pltpu.make_async_copy(source_rows, target_rows, sems.at[sem])

    stripes = [slice(i * STRIPE, (i + 1) * STRIPE) for i in range(STRIPES)]
    ids = [copy(cluster, clusters, 2 * STRIPES), copy(source, sources, 2 * STRIPES + 1)]
    arriving = [copy(embeddings.at[rows], raw.at[rows], i) for i, rows in enumerate(stripes)]
    leaving = [copy(unit.at[rows], out.at[rows], STRIPES + i) for i, rows in enumerate(stripes)]
    leaving.append(copy(unit.at[ROWS:], out.at[ROWS:], 2 * STRIPES + 2))
    for move in ids + arriving:
        move.start()
    for move in ids:
        move.wait()
    line = lax.broadcasted_iota(jnp.int32, (TAIL, ROWS), 0)
    number = sources[...].reshape(1, ROWS)
    rank = clusters[...].reshape(1, ROWS)
    tail = jnp.where(line == 0, rank, jnp.where(line == 1, number // 256, jnp.where(line == 2, number % 256, 0)))
    unit[ROWS:, :ROWS] = tail.astype(jnp.float32).astype(jnp.bfloat16)
    unit[ROWS:, ROWS:] = jnp.zeros((TAIL, WIDTH - ROWS), jnp.bfloat16)
    leaving[STRIPES].start()
    for i, rows in enumerate(stripes):
        arriving[i].wait()
        widened = raw[rows, :].astype(jnp.float32)
        factor = lax.rsqrt(jnp.mean(widened * widened, axis=1, keepdims=True) + 1e-06) / 32.0
        unit[rows, :] = (widened * factor).astype(jnp.bfloat16)
        leaving[i].start()
    for move in leaving:
        move.wait()


def prepare(embeddings, cluster_id, source_id):
    far = pl.BlockSpec(memory_space=pltpu.HBM)
    return pl.pallas_call(
        prepare_kernel,
        out_shape=jax.ShapeDtypeStruct((BLOCK, WIDTH), jnp.bfloat16),
        in_specs=[far] * 3,
        out_specs=far,
        scratch_shapes=[
            pltpu.VMEM((ROWS, WIDTH), jnp.bfloat16),
            pltpu.VMEM((ROWS,), jnp.int32),
            pltpu.VMEM((ROWS,), jnp.int32),
            pltpu.VMEM((BLOCK, WIDTH), jnp.bfloat16),
            pltpu.SemaphoreType.DMA((2 * STRIPES + 3,)),
        ],
        compiler_params=pltpu.CompilerParams(vmem_limit_bytes=60 << 20),
        name="prepare",
    )(embeddings, cluster_id, source_id)


def score_kernel(step, given, *refs):
    order = STEPS[step][0]
    n = len(order)
    results = targets(step)
    place = {b: i for i, b in enumerate(order)}
    blocks, refs = refs[:n], refs[n:]
    earlier, refs = dict(zip(given, refs)), refs[len(given) :]
    outs, refs = dict(zip(results, refs)), refs[len(results) :]
    held, ids, sems = refs
    copies = []
    for i, block in enumerate(blocks):
        copies.append(pltpu.make_async_copy(block.at[ROWS:], ids.at[i], sems.at[0, i]))
        copies.append(pltpu.make_async_copy(block.at[:ROWS], held.at[pl.ds(i * ROWS, ROWS)], sems.at[1, i]))
    for copy in copies:
        copy.start()
    for copy in copies:
        copy.wait()

    def word(b):
        parts = ids[place[b], :, :ROWS].astype(jnp.float32)
        return parts[0:1] * 65536.0 + parts[1:2] * 256.0 + parts[2:3]

    over_lanes, over_rows = {}, {}

    def update(table, b, value):
        table[b] = jnp.maximum(table[b], value) if b in table else value

    for rows, columns, sides in products(step):
        scores = lax.dot_general(
            held[place[rows[0]] * ROWS : (place[rows[-1]] + 1) * ROWS, :],
            held[place[columns[0]] * ROWS : (place[columns[-1]] + 1) * ROWS, :],
            (((1,), (1,)), ((), ())),
            preferred_element_type=jnp.float32,
        )
        for j, a in enumerate(rows):
            near = jnp.broadcast_to(word(a), (128, ROWS)).T.astype(jnp.int32)
            for i, b in enumerate(columns):
                far = word(b).astype(jnp.int32)
                down = []
                for k in range(ROWS // 128):
                    at = i * ROWS + k * 128
                    mixed = near ^ far[:, k * 128 : (k + 1) * 128]
                    partner = (mixed > 0) & (mixed < 65536)
                    kept = jnp.where(partner, scores[j * ROWS : (j + 1) * ROWS, at : at + 128], -1.0)
                    if a in sides:
                        update(over_lanes, a, kept)
                    down.append(jnp.max(kept.reshape(ROWS // 8, 8, 128), axis=0))
                if b in sides and b != a:
                    update(over_rows, b, jnp.concatenate(down, axis=1))

    for b in results:
        value = jnp.full((1, ROWS), -1.0, jnp.float32)
        if b in over_lanes:
            value = jnp.maximum(value, jnp.max(over_lanes[b].T, axis=0, keepdims=True))
        if b in over_rows:
            value = jnp.maximum(value, jnp.max(over_rows[b], axis=0, keepdims=True))
        if b in earlier:
            value = jnp.maximum(value, earlier[b][...])
        outs[b][...] = value


def score(step, blocks, earlier):
    order = STEPS[step][0]
    n = len(order)
    results = targets(step)
    given = tuple(b for b in results if b in earlier)
    pairs = sum(len(rows) * len(columns) for rows, columns, _ in products(step))
    vmem = pl.BlockSpec(memory_space=pltpu.VMEM)
    values = pl.pallas_call(
        functools.partial(score_kernel, step, given),
        out_shape=[jax.ShapeDtypeStruct((1, ROWS), jnp.float32)] * len(results),
        in_specs=[pl.BlockSpec(memory_space=pl.ANY)] * n + [vmem] * len(given),
        out_specs=[vmem] * len(results),
        scratch_shapes=[
            pltpu.VMEM((n * ROWS, WIDTH), jnp.bfloat16),
            pltpu.VMEM((n, TAIL, WIDTH), jnp.bfloat16),
            pltpu.SemaphoreType.DMA((2, n)),
        ],
        compiler_params=pltpu.CompilerParams(vmem_limit_bytes=28 << 20),
        cost_estimate=pl.CostEstimate(
            flops=2 * pairs * ROWS * ROWS * WIDTH, bytes_accessed=n * BLOCK * WIDTH * 2, transcendentals=0
        ),
        name="score_" + step,
    )(*[blocks[b] for b in order], *[earlier[b] for b in given])
    return {**earlier, **dict(zip(results, values))}


def local(embeddings, cluster_id, source_id):
    blocks = {0: prepare(embeddings, cluster_id, source_id)}
    for block, by in FIRST:
        blocks[block] = receive(blocks[0], by)
    for block, parent, by in SECOND:
        blocks[block] = receive(blocks[parent], by)
    best = score("early", blocks, {})
    best = score("middle", blocks, best)
    got = [receive(best[b], OFFSETS[b], back=True) for b in (3, 2)]
    best = score("late", blocks, best)
    got += [receive(best[b], OFFSETS[b], back=True) for b in (8, 4)]
    best = score("last", blocks, best)
    own = best[0]
    for value in got:
        own = jnp.maximum(own, value)
    return own.reshape(ROWS)


def solution(mesh):
    return jax.shard_map(
        local,
        mesh=mesh,
        in_specs=(P(("grp", "blk"), None), P(("grp", "blk")), P(("grp", "blk"))),
        out_specs=P(("grp", "blk")),
        check_vma=False,
    )
```

```python
import functools

import jax
import jax.numpy as jnp
from jax import lax
from jax.experimental import pallas as pl
from jax.experimental.pallas import tpu as pltpu
from jax.sharding import PartitionSpec as P

TORUS = (2, 4, 4)
OFFSETS = (
    (0, 0, 0),
    (0, 0, 3),
    (0, 1, 0),
    (0, 3, 1),
    (1, 0, 0),
    (0, 0, 2),
    (0, 2, 0),
    (0, 2, 2),
    (1, 0, 3),
)
FIRST = ((1, (0, 0, 3)), (2, (0, 1, 0)), (3, (0, 3, 1)), (4, (1, 0, 0)))
SECOND = ((8, 1, (1, 0, 0)), (5, 1, (0, 0, 3)), (6, 2, (0, 1, 0)), (7, 3, (0, 3, 1)))
ROWS = 384
TAIL = 16
BLOCK = ROWS + TAIL
WIDTH = 1024
STRIPE = 64
STRIPES = ROWS // STRIPE
STEPS = {
    "early": (
        (0, 1, 2, 3, 4),
        ((0, 0, 0, 4, (0, 2, 3)), (1, 1, 2, 4, (2, 3, 4)), (2, 2, 3, 4, (2, 3, 4)), (3, 3, 4, 4, (3, 4))),
    ),
    "middle": ((5, 0, 2, 3, 4), ((0, 0, 1, 4, (0, 2, 3, 4)),)),
    "second": ((8, 0, 2, 3, 4), ((0, 0, 1, 4, (2, 3, 8)),)),
    "late": ((8, 4, 6, 7), ((0, 1, 2, 3, (4, 8)),)),
    "last": ((0, 6, 7), ((0, 0, 1, 2, (0,)),)),
}


def difference(a, b):
    return tuple((p - q) % n for p, q, n in zip(a, b, TORUS))


def products(step):
    order, strips = STEPS[step]
    for first, last, left, right, sides in strips:
        yield order[first : last + 1], order[left : right + 1], sides


def targets(step):
    return tuple(sorted({b for rows, columns, sides in products(step) for b in sides if b in rows + columns}))


def check():
    met = set()
    for step in STEPS:
        for rows, columns, sides in products(step):
            for a in rows:
                for b in columns:
                    met |= {difference(OFFSETS[b], OFFSETS[a])} if a in sides else set()
                    met |= {difference(OFFSETS[a], OFFSETS[b])} if b in sides else set()
    assert len(met) == 32
    assert all(OFFSETS[block] == by for block, by in FIRST)
    assert all(difference(OFFSETS[block], OFFSETS[parent]) == by for block, parent, by in SECOND)


check()


def flat(y, z, x):
    return ((y % TORUS[0]) * TORUS[1] + z % TORUS[1]) * TORUS[2] + x % TORUS[2]


def receive(array, by, back=False):
    links = []
    for y in range(TORUS[0]):
        for z in range(TORUS[1]):
            for x in range(TORUS[2]):
                far, near = flat(y + by[0], z + by[1], x + by[2]), flat(y, z, x)
                links.append((near, far) if back else (far, near))
    return lax.ppermute(array, "blk", links)


def unit_rows(rows):
    widened = rows.astype(jnp.float32)
    factor = lax.rsqrt(jnp.mean(widened * widened, axis=1, keepdims=True) + 1e-06) / 32.0
    return (widened * factor).astype(jnp.bfloat16)


def prepare_kernel(embeddings, cluster, source, out, out_tail, raw, clusters, sources, unit, sems):
    def copy(source_rows, target_rows, sem):
        return pltpu.make_async_copy(source_rows, target_rows, sems.at[sem])

    stripes = [slice(i * STRIPE, (i + 1) * STRIPE) for i in range(STRIPES)]
    ids = [copy(cluster, clusters, 2 * STRIPES), copy(source, sources, 2 * STRIPES + 1)]
    arriving = [copy(embeddings.at[rows], raw.at[rows], i) for i, rows in enumerate(stripes)]
    leaving = [copy(unit.at[rows], out.at[rows], STRIPES + i) for i, rows in enumerate(stripes)]
    leaving.append(copy(unit.at[ROWS:], out.at[ROWS:], 2 * STRIPES + 2))
    leaving.append(copy(unit.at[ROWS:], out_tail, 2 * STRIPES + 3))
    for move in ids + arriving:
        move.start()
    for move in ids:
        move.wait()
    line = lax.broadcasted_iota(jnp.int32, (TAIL, ROWS), 0)
    number = sources[...].reshape(1, ROWS)
    rank = clusters[...].reshape(1, ROWS)
    tail = jnp.where(line == 0, rank, jnp.where(line == 1, number // 256, jnp.where(line == 2, number % 256, 0)))
    unit[ROWS:, :ROWS] = tail.astype(jnp.float32).astype(jnp.bfloat16)
    unit[ROWS:, ROWS:] = jnp.zeros((TAIL, WIDTH - ROWS), jnp.bfloat16)
    leaving[STRIPES].start()
    leaving[STRIPES + 1].start()
    for i, rows in enumerate(stripes):
        arriving[i].wait()
        unit[rows, :] = unit_rows(raw[rows, :])
        leaving[i].start()
    for move in leaving:
        move.wait()


def prepare(embeddings, cluster_id, source_id):
    far = pl.BlockSpec(memory_space=pltpu.HBM)
    return pl.pallas_call(
        prepare_kernel,
        out_shape=[jax.ShapeDtypeStruct((rows, WIDTH), jnp.bfloat16) for rows in (BLOCK, TAIL)],
        in_specs=[far] * 3,
        out_specs=[far] * 2,
        scratch_shapes=[
            pltpu.VMEM((ROWS, WIDTH), jnp.bfloat16),
            pltpu.VMEM((ROWS,), jnp.int32),
            pltpu.VMEM((ROWS,), jnp.int32),
            pltpu.VMEM((BLOCK, WIDTH), jnp.bfloat16),
            pltpu.SemaphoreType.DMA((2 * STRIPES + 4,)),
        ],
        compiler_params=pltpu.CompilerParams(vmem_limit_bytes=60 << 20),
        name="prepare",
    )(embeddings, cluster_id, source_id)


def join_kernel(raw, tail, out):
    for i in range(STRIPES):
        rows = slice(i * STRIPE, (i + 1) * STRIPE)
        out[rows, :] = unit_rows(raw[rows, :])
    out[ROWS:, :] = tail[...]


def join(raw, tail):
    vmem = pl.BlockSpec(memory_space=pltpu.VMEM)
    return pl.pallas_call(
        join_kernel,
        out_shape=jax.ShapeDtypeStruct((BLOCK, WIDTH), jnp.bfloat16),
        in_specs=[vmem] * 2,
        out_specs=vmem,
        compiler_params=pltpu.CompilerParams(vmem_limit_bytes=16 << 20),
        name="join",
    )(raw, tail)


def score_kernel(step, given, *refs):
    order = STEPS[step][0]
    n = len(order)
    results = targets(step)
    place = {b: i for i, b in enumerate(order)}
    blocks, refs = refs[:n], refs[n:]
    earlier, refs = dict(zip(given, refs)), refs[len(given) :]
    outs, refs = dict(zip(results, refs)), refs[len(results) :]
    held, ids, sems = refs
    copies = []
    for i, block in enumerate(blocks):
        copies.append(pltpu.make_async_copy(block.at[ROWS:], ids.at[i], sems.at[0, i]))
        copies.append(pltpu.make_async_copy(block.at[:ROWS], held.at[pl.ds(i * ROWS, ROWS)], sems.at[1, i]))
    for copy in copies:
        copy.start()
    for copy in copies:
        copy.wait()

    def word(b):
        parts = ids[place[b], :, :ROWS].astype(jnp.float32)
        return parts[0:1] * 65536.0 + parts[1:2] * 256.0 + parts[2:3]

    over_lanes, over_rows = {}, {}

    def update(table, b, value):
        table[b] = jnp.maximum(table[b], value) if b in table else value

    for rows, columns, sides in products(step):
        scores = lax.dot_general(
            held[place[rows[0]] * ROWS : (place[rows[-1]] + 1) * ROWS, :],
            held[place[columns[0]] * ROWS : (place[columns[-1]] + 1) * ROWS, :],
            (((1,), (1,)), ((), ())),
            preferred_element_type=jnp.float32,
        )
        for j, a in enumerate(rows):
            near = jnp.broadcast_to(word(a), (128, ROWS)).T.astype(jnp.int32)
            for i, b in enumerate(columns):
                far = word(b).astype(jnp.int32)
                down = []
                for k in range(ROWS // 128):
                    at = i * ROWS + k * 128
                    mixed = near ^ far[:, k * 128 : (k + 1) * 128]
                    partner = (mixed > 0) & (mixed < 65536)
                    kept = jnp.where(partner, scores[j * ROWS : (j + 1) * ROWS, at : at + 128], -1.0)
                    if a in sides:
                        update(over_lanes, a, kept)
                    down.append(jnp.max(kept.reshape(ROWS // 8, 8, 128), axis=0))
                if b in sides and b != a:
                    update(over_rows, b, jnp.concatenate(down, axis=1))

    for b in results:
        value = jnp.full((1, ROWS), -1.0, jnp.float32)
        if b in over_lanes:
            value = jnp.maximum(value, jnp.max(over_lanes[b].T, axis=0, keepdims=True))
        if b in over_rows:
            value = jnp.maximum(value, jnp.max(over_rows[b], axis=0, keepdims=True))
        if b in earlier:
            value = jnp.maximum(value, earlier[b][...])
        outs[b][...] = value


def score(step, blocks, earlier):
    order = STEPS[step][0]
    n = len(order)
    results = targets(step)
    given = tuple(b for b in results if b in earlier)
    pairs = sum(len(rows) * len(columns) for rows, columns, _ in products(step))
    vmem = pl.BlockSpec(memory_space=pltpu.VMEM)
    values = pl.pallas_call(
        functools.partial(score_kernel, step, given),
        out_shape=[jax.ShapeDtypeStruct((1, ROWS), jnp.float32)] * len(results),
        in_specs=[pl.BlockSpec(memory_space=pl.ANY)] * n + [vmem] * len(given),
        out_specs=[vmem] * len(results),
        scratch_shapes=[
            pltpu.VMEM((n * ROWS, WIDTH), jnp.bfloat16),
            pltpu.VMEM((n, TAIL, WIDTH), jnp.bfloat16),
            pltpu.SemaphoreType.DMA((2, n)),
        ],
        compiler_params=pltpu.CompilerParams(vmem_limit_bytes=28 << 20),
        cost_estimate=pl.CostEstimate(
            flops=2 * pairs * ROWS * ROWS * WIDTH, bytes_accessed=n * BLOCK * WIDTH * 2, transcendentals=0
        ),
        name="score_" + step,
    )(*[blocks[b] for b in order], *[earlier[b] for b in given])
    return {**earlier, **dict(zip(results, values))}


def local(embeddings, cluster_id, source_id):
    whole, tail = prepare(embeddings, cluster_id, source_id)
    blocks = {0: whole}
    for block, by in FIRST:
        if block == 1:
            blocks[block] = join(receive(embeddings, by), receive(tail, by))
        else:
            blocks[block] = receive(whole, by)
    for block, parent, by in SECOND:
        blocks[block] = receive(blocks[parent], by)
    best = score("early", blocks, {})
    best = score("middle", blocks, best)
    best = score("second", blocks, best)
    got = [receive(best[b], OFFSETS[b], back=True) for b in (3, 2)]
    best = score("late", blocks, best)
    got += [receive(best[b], OFFSETS[b], back=True) for b in (8, 4)]
    best = score("last", blocks, best)
    own = best[0]
    for value in got:
        own = jnp.maximum(own, value)
    return own.reshape(ROWS)


def solution(mesh):
    return jax.shard_map(
        local,
        mesh=mesh,
        in_specs=(P(("grp", "blk"), None), P(("grp", "blk")), P(("grp", "blk"))),
        out_specs=P(("grp", "blk")),
        check_vma=False,
    )
```

```python
import functools

import jax
import jax.numpy as jnp
from jax import lax
from jax.experimental import pallas as pl
from jax.experimental.pallas import tpu as pltpu
from jax.sharding import PartitionSpec as P

TORUS = (2, 4, 4)
OFFSETS = (
    (0, 0, 0),
    (0, 0, 3),
    (0, 1, 0),
    (0, 3, 1),
    (1, 0, 0),
    (0, 0, 2),
    (0, 2, 0),
    (0, 2, 2),
    (1, 0, 3),
)
FIRST = ((1, (0, 0, 3)), (2, (0, 1, 0)), (3, (0, 3, 1)), (4, (1, 0, 0)))
SECOND = ((8, 1, (1, 0, 0)), (5, 1, (0, 0, 3)), (6, 2, (0, 1, 0)), (7, 3, (0, 3, 1)))
ROWS = 384
TAIL = 16
BLOCK = ROWS + TAIL
WIDTH = 1024
STRIPE = 128
STRIPES = ROWS // STRIPE
PACKED = (1, 0, 2, 3, 4)
STEPS = {
    "early": (
        (),
        PACKED,
        ((0, PACKED, (0, 2, 3)), (1, (2, 3, 4), (2, 3, 4)), (2, (3, 4), (2, 3, 4)), (3, (4,), (3, 4))),
    ),
    "middle": ((5,), (), ((5, (2, 3, 4), (2, 3, 4)),)),
    "second": ((8,), (), ((8, (0, 2, 3, 4), (2, 3, 8)),)),
    "late": ((8,), (7, 6), ((8, (7, 6), (8,)), (4, (7, 6), (4,)))),
    "last": ((), (5, 7, 6), ((0, (5, 7, 6), (0,)),)),
}


def difference(a, b):
    return tuple((p - q) % n for p, q, n in zip(a, b, TORUS))


def targets(step):
    return tuple(sorted({b for a, others, sides in STEPS[step][2] for b in sides if b in (a, *others)}))


def check():
    met = set()
    for _, _, strips in STEPS.values():
        for a, others, sides in strips:
            for b in others:
                met |= {difference(OFFSETS[b], OFFSETS[a])} if a in sides else set()
                met |= {difference(OFFSETS[a], OFFSETS[b])} if b in sides else set()
    assert len(met) == 32
    assert all(OFFSETS[block] == by for block, by in FIRST)
    assert all(difference(OFFSETS[block], OFFSETS[parent]) == by for block, parent, by in SECOND)


check()


def flat(y, z, x):
    return ((y % TORUS[0]) * TORUS[1] + z % TORUS[1]) * TORUS[2] + x % TORUS[2]


def receive(array, by, back=False):
    links = []
    for y in range(TORUS[0]):
        for z in range(TORUS[1]):
            for x in range(TORUS[2]):
                far, near = flat(y + by[0], z + by[1], x + by[2]), flat(y, z, x)
                links.append((near, far) if back else (far, near))
    return lax.ppermute(array, "blk", links)


def unit_rows(rows):
    widened = rows.astype(jnp.float32)
    factor = lax.rsqrt(jnp.mean(widened * widened, axis=1, keepdims=True) + 1e-06) / 32.0
    return (widened * factor).astype(jnp.bfloat16)


def prepare_kernel(embeddings, cluster, source, out, out_tail, raw, clusters, sources, unit, sems):
    def copy(source_rows, target_rows, sem):
        return pltpu.make_async_copy(source_rows, target_rows, sems.at[sem])

    stripes = [slice(i * STRIPE, (i + 1) * STRIPE) for i in range(STRIPES)]
    ids = [copy(cluster, clusters, 2 * STRIPES), copy(source, sources, 2 * STRIPES + 1)]
    arriving = [copy(embeddings.at[rows], raw.at[rows], i) for i, rows in enumerate(stripes)]
    leaving = [copy(unit.at[rows], out.at[rows], STRIPES + i) for i, rows in enumerate(stripes)]
    leaving.append(copy(unit.at[ROWS:], out.at[ROWS:], 2 * STRIPES + 2))
    leaving.append(copy(unit.at[ROWS:], out_tail, 2 * STRIPES + 3))
    for move in ids + arriving:
        move.start()
    for move in ids:
        move.wait()
    line = lax.broadcasted_iota(jnp.int32, (TAIL, ROWS), 0)
    number = sources[...].reshape(1, ROWS)
    rank = clusters[...].reshape(1, ROWS)
    tail = jnp.where(line == 0, rank, jnp.where(line == 1, number // 256, jnp.where(line == 2, number % 256, 0)))
    unit[ROWS:, :ROWS] = tail.astype(jnp.float32).astype(jnp.bfloat16)
    unit[ROWS:, ROWS:] = jnp.zeros((TAIL, WIDTH - ROWS), jnp.bfloat16)
    leaving[STRIPES].start()
    leaving[STRIPES + 1].start()
    for i, rows in enumerate(stripes):
        arriving[i].wait()
        unit[rows, :] = unit_rows(raw[rows, :])
        leaving[i].start()
    for move in leaving:
        move.wait()


def prepare(embeddings, cluster_id, source_id):
    far = pl.BlockSpec(memory_space=pltpu.HBM)
    return pl.pallas_call(
        prepare_kernel,
        out_shape=[jax.ShapeDtypeStruct((rows, WIDTH), jnp.bfloat16) for rows in (BLOCK, TAIL)],
        in_specs=[far] * 3,
        out_specs=[far] * 2,
        scratch_shapes=[
            pltpu.VMEM((ROWS, WIDTH), jnp.bfloat16),
            pltpu.VMEM((ROWS,), jnp.int32),
            pltpu.VMEM((ROWS,), jnp.int32),
            pltpu.VMEM((BLOCK, WIDTH), jnp.bfloat16),
            pltpu.SemaphoreType.DMA((2 * STRIPES + 4,)),
        ],
        compiler_params=pltpu.CompilerParams(vmem_limit_bytes=60 << 20),
        name="prepare",
    )(embeddings, cluster_id, source_id)


def join_kernel(raw, tail, out):
    for i in range(STRIPES):
        rows = slice(i * STRIPE, (i + 1) * STRIPE)
        out[rows, :] = unit_rows(raw[rows, :])
    out[ROWS:, :] = tail[...]


def join(raw, tail):
    vmem = pl.BlockSpec(memory_space=pltpu.VMEM)
    return pl.pallas_call(
        join_kernel,
        out_shape=jax.ShapeDtypeStruct((BLOCK, WIDTH), jnp.bfloat16),
        in_specs=[vmem] * 2,
        out_specs=vmem,
        compiler_params=pltpu.CompilerParams(vmem_limit_bytes=16 << 20),
        name="join",
    )(raw, tail)


def score_kernel(step, given, *refs):
    direct, joined, strips = STEPS[step]
    results = targets(step)
    first = step == "early"
    refs = list(refs)

    def take(count):
        taken, refs[:count] = refs[:count], []
        return taken

    in_place = dict(zip(direct, take(len(direct))))
    sources = take(len(joined))
    packed, packed_ids = (None, None) if first else take(2)
    earlier = dict(zip(given, take(len(given))))
    outs = dict(zip(results, take(len(results))))
    if joined:
        held, ids = take(2)
        (sems,) = take(1)
        copies = []
        for i, block in enumerate(sources):
            copies.append(pltpu.make_async_copy(block.at[ROWS:], ids.at[i], sems.at[0, i]))
            copies.append(pltpu.make_async_copy(block.at[:ROWS], held.at[pl.ds(i * ROWS, ROWS)], sems.at[1, i]))
        for copy in copies:
            copy.start()
        for copy in copies:
            copy.wait()

    def rows_of(blocks):
        b, n = blocks[0], len(blocks)
        if b in in_place:
            return in_place[b][:ROWS, :]
        order, ref = (joined, held) if b in joined else (PACKED, packed)
        at = order.index(b)
        assert order[at : at + n] == tuple(blocks)
        return ref[at * ROWS : (at + n) * ROWS, :]

    def word(b):
        if b in in_place:
            parts = in_place[b][ROWS:, :ROWS]
        elif b in joined:
            parts = ids[joined.index(b), :, :ROWS]
        else:
            parts = packed_ids[PACKED.index(b), :, :ROWS]
        parts = parts.astype(jnp.float32)
        return parts[0:1] * 65536.0 + parts[1:2] * 256.0 + parts[2:3]

    over_lanes, over_rows = {}, {}

    def update(table, b, value):
        table[b] = jnp.maximum(table[b], value) if b in table else value

    for a, others, sides in strips:
        scores = lax.dot_general(
            rows_of((a,)), rows_of(others), (((1,), (1,)), ((), ())), preferred_element_type=jnp.float32
        )
        near = jnp.broadcast_to(word(a), (128, ROWS)).T.astype(jnp.int32)
        for i, b in enumerate(others):
            far = word(b).astype(jnp.int32)
            down = []
            for k in range(ROWS // 128):
                at = i * ROWS + k * 128
                mixed = near ^ far[:, k * 128 : (k + 1) * 128]
                partner = (mixed > 0) & (mixed < 65536)
                kept = jnp.where(partner, scores[:, at : at + 128], -1.0)
                if a in sides:
                    update(over_lanes, a, kept)
                down.append(jnp.max(kept.reshape(ROWS // 8, 8, 128), axis=0))
            if b in sides and b != a:
                update(over_rows, b, jnp.concatenate(down, axis=1))

    for b in results:
        value = jnp.full((1, ROWS), -1.0, jnp.float32)
        if b in over_lanes:
            value = jnp.maximum(value, jnp.max(over_lanes[b].T, axis=0, keepdims=True))
        if b in over_rows:
            value = jnp.maximum(value, jnp.max(over_rows[b], axis=0, keepdims=True))
        if b in earlier:
            value = jnp.maximum(value, earlier[b][...])
        outs[b][...] = value


def score(step, blocks, earlier, packed=()):
    direct, joined, strips = STEPS[step]
    results = targets(step)
    given = tuple(b for b in results if b in earlier)
    n = len(joined)
    first = step == "early"
    pairs = sum(len(others) for _, others, _ in strips)
    vmem, free = pl.BlockSpec(memory_space=pltpu.VMEM), pl.BlockSpec(memory_space=pl.ANY)
    shapes = [((n * ROWS, WIDTH), jnp.bfloat16), ((n, TAIL, WIDTH), jnp.bfloat16)] if n else []
    values = pl.pallas_call(
        functools.partial(score_kernel, step, given),
        out_shape=[jax.ShapeDtypeStruct((1, ROWS), jnp.float32)] * len(results)
        + [jax.ShapeDtypeStruct(*shape) for shape in shapes if first],
        in_specs=[vmem] * len(direct) + [free] * n + [vmem] * (len(packed) + len(given)),
        out_specs=[vmem] * (len(results) + (len(shapes) if first else 0)),
        scratch_shapes=[pltpu.VMEM(*shape) for shape in shapes if not first]
        + ([pltpu.SemaphoreType.DMA((2, n))] if n else []),
        compiler_params=pltpu.CompilerParams(vmem_limit_bytes=28 << 20),
        cost_estimate=pl.CostEstimate(
            flops=2 * pairs * ROWS * ROWS * WIDTH, bytes_accessed=2 * pairs * ROWS * WIDTH, transcendentals=0
        ),
        name="score_" + step,
    )(*[blocks[b] for b in direct + joined], *packed, *[earlier[b] for b in given])
    return {**earlier, **dict(zip(results, values))}, values[len(results) :]


def local(embeddings, cluster_id, source_id):
    whole, tail = prepare(embeddings, cluster_id, source_id)
    blocks = {0: whole}
    for block, by in FIRST:
        if block == 1:
            blocks[block] = join(receive(embeddings, by), receive(tail, by))
        else:
            blocks[block] = receive(whole, by)
    for block, parent, by in SECOND:
        whole = blocks[parent]
        if block == 7:
            whole, blocks[4] = lax.optimization_barrier((whole, blocks[4]))
        blocks[block] = receive(whole, by)
    best, packed = score("early", blocks, {})
    best, _ = score("middle", blocks, best, packed)
    best, _ = score("second", blocks, best, packed)
    got = [receive(best[b], OFFSETS[b], back=True) for b in (2, 3)]
    best, _ = score("late", blocks, best, packed)
    got += [receive(best[b], OFFSETS[b], back=True) for b in (8, 4)]
    best, _ = score("last", blocks, best, packed)
    own = best[0]
    for value in got:
        own = jnp.maximum(own, value)
    return own.reshape(ROWS)


def solution(mesh):
    return jax.shard_map(
        local,
        mesh=mesh,
        in_specs=(P(("grp", "blk"), None), P(("grp", "blk")), P(("grp", "blk"))),
        out_specs=P(("grp", "blk")),
        check_vma=False,
    )
```

```python
import functools

import jax
import jax.numpy as jnp
from jax import lax
from jax.experimental import pallas as pl
from jax.experimental.pallas import tpu as pltpu
from jax.sharding import PartitionSpec as P

TORUS = (2, 4, 4)
OFFSETS = (
    (0, 0, 0),
    (0, 0, 3),
    (0, 1, 0),
    (0, 3, 1),
    (1, 0, 0),
    (0, 0, 2),
    (0, 2, 0),
    (0, 2, 2),
    (1, 0, 3),
)
FIRST = ((1, (0, 0, 3)), (2, (0, 1, 0)), (3, (0, 3, 1)), (4, (1, 0, 0)))
SECOND = ((8, 1, (1, 0, 0)), (5, 1, (0, 0, 3)), (6, 2, (0, 1, 0)), (7, 3, (0, 3, 1)))
ROWS = 384
TAIL = 16
BLOCK = ROWS + TAIL
WIDTH = 1024
STRIPE = 128
STRIPES = ROWS // STRIPE
PACKED = (1, 0, 2, 3, 4)
STEPS = {
    "early": (
        (),
        PACKED,
        ((0, PACKED, (0, 2, 3)), (1, (2, 3, 4), (2, 3, 4)), (2, (3, 4), (2, 3, 4)), (3, (4,), (3, 4))),
    ),
    "middle": ((5,), (), ((5, (2, 3, 4), (2, 3, 4)),)),
    "second": ((8,), (), ((8, (0, 2, 3, 4), (2, 3, 8)),)),
    "late": ((8,), (7, 6), ((8, (7, 6), (8,)), (4, (7, 6), (4,)))),
    "last": ((), (5, 7, 6), ((0, (5, 7, 6), (0,)),)),
}


def difference(a, b):
    return tuple((p - q) % n for p, q, n in zip(a, b, TORUS))


def targets(step):
    return tuple(sorted({b for a, others, sides in STEPS[step][2] for b in sides if b in (a, *others)}))


def check():
    met = set()
    for _, _, strips in STEPS.values():
        for a, others, sides in strips:
            for b in others:
                met |= {difference(OFFSETS[b], OFFSETS[a])} if a in sides else set()
                met |= {difference(OFFSETS[a], OFFSETS[b])} if b in sides else set()
    assert len(met) == 32
    assert all(OFFSETS[block] == by for block, by in FIRST)
    assert all(difference(OFFSETS[block], OFFSETS[parent]) == by for block, parent, by in SECOND)


check()


def flat(y, z, x):
    return ((y % TORUS[0]) * TORUS[1] + z % TORUS[1]) * TORUS[2] + x % TORUS[2]


def receive(array, by, back=False):
    links = []
    for y in range(TORUS[0]):
        for z in range(TORUS[1]):
            for x in range(TORUS[2]):
                far, near = flat(y + by[0], z + by[1], x + by[2]), flat(y, z, x)
                links.append((near, far) if back else (far, near))
    return lax.ppermute(array, "blk", links)


def unit_rows(rows):
    widened = rows.astype(jnp.float32)
    factor = lax.rsqrt(jnp.mean(widened * widened, axis=1, keepdims=True) + 1e-06) / 32.0
    return (widened * factor).astype(jnp.bfloat16)


def prepare_kernel(embeddings, cluster, source, out, out_tail, raw, clusters, sources, unit, short, sems):
    def copy(source_rows, target_rows, sem):
        return pltpu.make_async_copy(source_rows, target_rows, sems.at[sem])

    stripes = [slice(i * STRIPE, (i + 1) * STRIPE) for i in range(STRIPES)]
    ids = [copy(cluster, clusters, 2 * STRIPES), copy(source, sources, 2 * STRIPES + 1)]
    arriving = [copy(embeddings.at[rows], raw.at[rows], i) for i, rows in enumerate(stripes)]
    leaving = [copy(unit.at[rows], out.at[rows], STRIPES + i) for i, rows in enumerate(stripes)]
    leaving.append(copy(unit.at[ROWS:], out.at[ROWS:], 2 * STRIPES + 2))
    leaving.append(copy(short, out_tail, 2 * STRIPES + 3))
    for move in ids + arriving:
        move.start()
    for move in ids:
        move.wait()
    line = lax.broadcasted_iota(jnp.int32, (TAIL, ROWS), 0)
    number = sources[...].reshape(1, ROWS)
    rank = clusters[...].reshape(1, ROWS)
    tail = jnp.where(line == 0, rank, jnp.where(line == 1, number // 256, jnp.where(line == 2, number % 256, 0)))
    tail = tail.astype(jnp.float32)
    unit[ROWS:, :ROWS] = tail.astype(jnp.bfloat16)
    pieces = [tail[i : i + 1, k * 128 : (k + 1) * 128] for i in range(3) for k in range(ROWS // 128)]
    pieces.append(jnp.zeros((TAIL - len(pieces), 128), jnp.float32))
    short[...] = jnp.concatenate(pieces, axis=0).astype(jnp.bfloat16)
    unit[ROWS:, ROWS:] = jnp.zeros((TAIL, WIDTH - ROWS), jnp.bfloat16)
    leaving[STRIPES].start()
    leaving[STRIPES + 1].start()
    for i, rows in enumerate(stripes):
        arriving[i].wait()
        unit[rows, :] = unit_rows(raw[rows, :])
        leaving[i].start()
    for move in leaving:
        move.wait()


def prepare(embeddings, cluster_id, source_id):
    far = pl.BlockSpec(memory_space=pltpu.HBM)
    return pl.pallas_call(
        prepare_kernel,
        out_shape=[jax.ShapeDtypeStruct(shape, jnp.bfloat16) for shape in ((BLOCK, WIDTH), (TAIL, 128))],
        in_specs=[far] * 3,
        out_specs=[far] * 2,
        scratch_shapes=[
            pltpu.VMEM((ROWS, WIDTH), jnp.bfloat16),
            pltpu.VMEM((ROWS,), jnp.int32),
            pltpu.VMEM((ROWS,), jnp.int32),
            pltpu.VMEM((BLOCK, WIDTH), jnp.bfloat16),
            pltpu.VMEM((TAIL, 128), jnp.bfloat16),
            pltpu.SemaphoreType.DMA((2 * STRIPES + 4,)),
        ],
        compiler_params=pltpu.CompilerParams(vmem_limit_bytes=60 << 20),
        name="prepare",
    )(embeddings, cluster_id, source_id)


def join_kernel(raw, tail, out):
    for i in range(STRIPES):
        rows = slice(i * STRIPE, (i + 1) * STRIPE)
        out[rows, :] = unit_rows(raw[rows, :])
    short = tail[...].astype(jnp.float32)
    n = ROWS // 128
    lines = [jnp.concatenate([short[i * n + k : i * n + k + 1] for k in range(n)], axis=1) for i in range(3)]
    lines.append(jnp.zeros((TAIL - 3, ROWS), jnp.float32))
    out[ROWS:, :ROWS] = jnp.concatenate(lines, axis=0).astype(jnp.bfloat16)
    out[ROWS:, ROWS:] = jnp.zeros((TAIL, WIDTH - ROWS), jnp.bfloat16)


def join(raw, tail):
    vmem = pl.BlockSpec(memory_space=pltpu.VMEM)
    return pl.pallas_call(
        join_kernel,
        out_shape=jax.ShapeDtypeStruct((BLOCK, WIDTH), jnp.bfloat16),
        in_specs=[vmem] * 2,
        out_specs=vmem,
        compiler_params=pltpu.CompilerParams(vmem_limit_bytes=16 << 20),
        name="join",
    )(raw, tail)


def score_kernel(step, given, *refs):
    direct, joined, strips = STEPS[step]
    results = targets(step)
    first = step == "early"
    refs = list(refs)

    def take(count):
        taken, refs[:count] = refs[:count], []
        return taken

    in_place = dict(zip(direct, take(len(direct))))
    sources = take(len(joined))
    packed, packed_ids = (None, None) if first else take(2)
    earlier = dict(zip(given, take(len(given))))
    outs = dict(zip(results, take(len(results))))
    if joined:
        held, ids = take(2)
        (sems,) = take(1)
        copies = []
        for i, block in enumerate(sources):
            copies.append(pltpu.make_async_copy(block.at[ROWS:], ids.at[i], sems.at[0, i]))
            copies.append(pltpu.make_async_copy(block.at[:ROWS], held.at[pl.ds(i * ROWS, ROWS)], sems.at[1, i]))
        for copy in copies:
            copy.start()
        for copy in copies:
            copy.wait()

    def rows_of(blocks):
        b, n = blocks[0], len(blocks)
        if b in in_place:
            return in_place[b][:ROWS, :]
        order, ref = (joined, held) if b in joined else (PACKED, packed)
        at = order.index(b)
        assert order[at : at + n] == tuple(blocks)
        return ref[at * ROWS : (at + n) * ROWS, :]

    def word(b):
        if b in in_place:
            parts = in_place[b][ROWS:, :ROWS]
        elif b in joined:
            parts = ids[joined.index(b), :, :ROWS]
        else:
            parts = packed_ids[PACKED.index(b), :, :ROWS]
        parts = parts.astype(jnp.float32)
        return parts[0:1] * 65536.0 + parts[1:2] * 256.0 + parts[2:3]

    over_lanes, over_rows = {}, {}

    def update(table, b, value):
        table[b] = jnp.maximum(table[b], value) if b in table else value

    for a, others, sides in strips:
        scores = lax.dot_general(
            rows_of((a,)), rows_of(others), (((1,), (1,)), ((), ())), preferred_element_type=jnp.float32
        )
        near = jnp.broadcast_to(word(a), (128, ROWS)).T.astype(jnp.int32)
        for i, b in enumerate(others):
            far = word(b).astype(jnp.int32)
            down = []
            for k in range(ROWS // 128):
                at = i * ROWS + k * 128
                mixed = near ^ far[:, k * 128 : (k + 1) * 128]
                partner = (mixed > 0) & (mixed < 65536)
                kept = jnp.where(partner, scores[:, at : at + 128], -1.0)
                if a in sides:
                    update(over_lanes, a, kept)
                down.append(jnp.max(kept.reshape(ROWS // 8, 8, 128), axis=0))
            if b in sides and b != a:
                update(over_rows, b, jnp.concatenate(down, axis=1))

    for b in results:
        value = jnp.full((1, ROWS), -1.0, jnp.float32)
        if b in over_lanes:
            value = jnp.maximum(value, jnp.max(over_lanes[b].T, axis=0, keepdims=True))
        if b in over_rows:
            value = jnp.maximum(value, jnp.max(over_rows[b], axis=0, keepdims=True))
        if b in earlier:
            value = jnp.maximum(value, earlier[b][...])
        outs[b][...] = value


def score(step, blocks, earlier, packed=()):
    direct, joined, strips = STEPS[step]
    results = targets(step)
    given = tuple(b for b in results if b in earlier)
    n = len(joined)
    first = step == "early"
    pairs = sum(len(others) for _, others, _ in strips)
    vmem, free = pl.BlockSpec(memory_space=pltpu.VMEM), pl.BlockSpec(memory_space=pl.ANY)
    shapes = [((n * ROWS, WIDTH), jnp.bfloat16), ((n, TAIL, WIDTH), jnp.bfloat16)] if n else []
    values = pl.pallas_call(
        functools.partial(score_kernel, step, given),
        out_shape=[jax.ShapeDtypeStruct((1, ROWS), jnp.float32)] * len(results)
        + [jax.ShapeDtypeStruct(*shape) for shape in shapes if first],
        in_specs=[vmem] * len(direct) + [free] * n + [vmem] * (len(packed) + len(given)),
        out_specs=[vmem] * (len(results) + (len(shapes) if first else 0)),
        scratch_shapes=[pltpu.VMEM(*shape) for shape in shapes if not first]
        + ([pltpu.SemaphoreType.DMA((2, n))] if n else []),
        compiler_params=pltpu.CompilerParams(vmem_limit_bytes=28 << 20),
        cost_estimate=pl.CostEstimate(
            flops=2 * pairs * ROWS * ROWS * WIDTH, bytes_accessed=2 * pairs * ROWS * WIDTH, transcendentals=0
        ),
        name="score_" + step,
    )(*[blocks[b] for b in direct + joined], *packed, *[earlier[b] for b in given])
    return {**earlier, **dict(zip(results, values))}, values[len(results) :]


def local(embeddings, cluster_id, source_id):
    whole, tail = prepare(embeddings, cluster_id, source_id)
    blocks = {0: whole}
    for block, by in FIRST:
        if block == 1:
            blocks[block] = join(receive(embeddings, by), receive(tail, by))
        else:
            blocks[block] = receive(whole, by)
    for block, parent, by in SECOND:
        whole = blocks[parent]
        if block == 7:
            whole, blocks[4] = lax.optimization_barrier((whole, blocks[4]))
        blocks[block] = receive(whole, by)
    best, packed = score("early", blocks, {})
    best, _ = score("middle", blocks, best, packed)
    best, _ = score("second", blocks, best, packed)
    got = [receive(best[b], OFFSETS[b], back=True) for b in (2, 3)]
    best, _ = score("late", blocks, best, packed)
    got += [receive(best[b], OFFSETS[b], back=True) for b in (8, 4)]
    best, _ = score("last", blocks, best, packed)
    own = best[0]
    for value in got:
        own = jnp.maximum(own, value)
    return own.reshape(ROWS)


def solution(mesh):
    return jax.shard_map(
        local,
        mesh=mesh,
        in_specs=(P(("grp", "blk"), None), P(("grp", "blk")), P(("grp", "blk"))),
        out_specs=P(("grp", "blk")),
        check_vma=False,
    )
```

```python
import functools

import jax
import jax.numpy as jnp
from jax import lax
from jax.experimental import pallas as pl
from jax.experimental.pallas import tpu as pltpu
from jax.sharding import PartitionSpec as P

TORUS = (2, 4, 4)
OFFSETS = (
    (0, 0, 0),
    (0, 0, 3),
    (0, 1, 0),
    (0, 3, 1),
    (1, 0, 0),
    (0, 0, 2),
    (0, 2, 0),
    (0, 2, 2),
    (1, 0, 3),
)
FIRST = ((1, (0, 0, 3)), (2, (0, 1, 0)), (3, (0, 3, 1)), (4, (1, 0, 0)))
SECOND = ((8, 1, (1, 0, 0)), (5, 1, (0, 0, 3)), (6, 2, (0, 1, 0)), (7, 3, (0, 3, 1)))
ROWS = 384
TAIL = 16
BLOCK = ROWS + TAIL
WIDTH = 1024
STRIPE = 192
STRIPES = ROWS // STRIPE
PACKED = (1, 0, 2, 3, 4)
PAIR = (8, 4)
STEPS = {
    "early": (
        (),
        PACKED,
        ((0, PACKED, (0, 2, 3)), (1, (2, 3, 4), (2, 3, 4)), (2, (3, 4), (2, 3, 4)), (3, (4,), (3, 4))),
    ),
    "middle": ((5,), (), ((5, (2, 3, 4), (2, 3, 4)),)),
    "second": ((8,), (), ((8, (0, 2, 3, 4), (2, 3, 8)),)),
    "late": ((6, 7), (), ((7, PAIR, PAIR), (6, PAIR, PAIR))),
    "last": ((), (5, 7, 6), ((0, (5, 7, 6), (0,)),)),
}


def difference(a, b):
    return tuple((p - q) % n for p, q, n in zip(a, b, TORUS))


def targets(step):
    return tuple(sorted({b for a, others, sides in STEPS[step][2] for b in sides if b in (a, *others)}))


def check():
    met = set()
    for _, _, strips in STEPS.values():
        for a, others, sides in strips:
            for b in others:
                met |= {difference(OFFSETS[b], OFFSETS[a])} if a in sides else set()
                met |= {difference(OFFSETS[a], OFFSETS[b])} if b in sides else set()
    assert len(met) == 32
    assert all(OFFSETS[block] == by for block, by in FIRST)
    assert all(difference(OFFSETS[block], OFFSETS[parent]) == by for block, parent, by in SECOND)


check()


def flat(y, z, x):
    return ((y % TORUS[0]) * TORUS[1] + z % TORUS[1]) * TORUS[2] + x % TORUS[2]


def receive(array, by, back=False):
    links = []
    for y in range(TORUS[0]):
        for z in range(TORUS[1]):
            for x in range(TORUS[2]):
                far, near = flat(y + by[0], z + by[1], x + by[2]), flat(y, z, x)
                links.append((near, far) if back else (far, near))
    return lax.ppermute(array, "blk", links)


def unit_rows(rows):
    widened = rows.astype(jnp.float32)
    factor = lax.rsqrt(jnp.mean(widened * widened, axis=1, keepdims=True) + 1e-06) / 32.0
    return (widened * factor).astype(jnp.bfloat16)


def prepare_kernel(embeddings, cluster, source, out, out_tail, raw, clusters, sources, unit, short, sems):
    def copy(source_rows, target_rows, sem):
        return pltpu.make_async_copy(source_rows, target_rows, sems.at[sem])

    stripes = [slice(i * STRIPE, (i + 1) * STRIPE) for i in range(STRIPES)]
    ids = [copy(cluster, clusters, 2 * STRIPES), copy(source, sources, 2 * STRIPES + 1)]
    arriving = [copy(embeddings.at[rows], raw.at[rows], i) for i, rows in enumerate(stripes)]
    leaving = [copy(unit.at[rows], out.at[rows], STRIPES + i) for i, rows in enumerate(stripes)]
    leaving.append(copy(unit.at[ROWS:], out.at[ROWS:], 2 * STRIPES + 2))
    leaving.append(copy(short, out_tail, 2 * STRIPES + 3))
    for move in ids + arriving:
        move.start()
    for move in ids:
        move.wait()
    line = lax.broadcasted_iota(jnp.int32, (TAIL, ROWS), 0)
    number = sources[...].reshape(1, ROWS)
    rank = clusters[...].reshape(1, ROWS)
    tail = jnp.where(line == 0, rank, jnp.where(line == 1, number // 256, jnp.where(line == 2, number % 256, 0)))
    tail = tail.astype(jnp.float32)
    unit[ROWS:, :ROWS] = tail.astype(jnp.bfloat16)
    pieces = [tail[i : i + 1, k * 128 : (k + 1) * 128] for i in range(3) for k in range(ROWS // 128)]
    pieces.append(jnp.zeros((TAIL - len(pieces), 128), jnp.float32))
    short[...] = jnp.concatenate(pieces, axis=0).astype(jnp.bfloat16)
    unit[ROWS:, ROWS:] = jnp.zeros((TAIL, WIDTH - ROWS), jnp.bfloat16)
    leaving[STRIPES].start()
    leaving[STRIPES + 1].start()
    for i, rows in enumerate(stripes):
        arriving[i].wait()
        unit[rows, :] = unit_rows(raw[rows, :])
        leaving[i].start()
    for move in leaving:
        move.wait()


def prepare(embeddings, cluster_id, source_id):
    far = pl.BlockSpec(memory_space=pltpu.HBM)
    return pl.pallas_call(
        prepare_kernel,
        out_shape=[jax.ShapeDtypeStruct(shape, jnp.bfloat16) for shape in ((BLOCK, WIDTH), (TAIL, 128))],
        in_specs=[far] * 3,
        out_specs=[far] * 2,
        scratch_shapes=[
            pltpu.VMEM((ROWS, WIDTH), jnp.bfloat16),
            pltpu.VMEM((ROWS,), jnp.int32),
            pltpu.VMEM((ROWS,), jnp.int32),
            pltpu.VMEM((BLOCK, WIDTH), jnp.bfloat16),
            pltpu.VMEM((TAIL, 128), jnp.bfloat16),
            pltpu.SemaphoreType.DMA((2 * STRIPES + 4,)),
        ],
        compiler_params=pltpu.CompilerParams(vmem_limit_bytes=60 << 20),
        name="prepare",
    )(embeddings, cluster_id, source_id)


def join_kernel(raw, tail, out):
    for i in range(STRIPES):
        rows = slice(i * STRIPE, (i + 1) * STRIPE)
        out[rows, :] = unit_rows(raw[rows, :])
    short = tail[...].astype(jnp.float32)
    n = ROWS // 128
    lines = [jnp.concatenate([short[i * n + k : i * n + k + 1] for k in range(n)], axis=1) for i in range(3)]
    lines.append(jnp.zeros((TAIL - 3, ROWS), jnp.float32))
    out[ROWS:, :ROWS] = jnp.concatenate(lines, axis=0).astype(jnp.bfloat16)
    out[ROWS:, ROWS:] = jnp.zeros((TAIL, WIDTH - ROWS), jnp.bfloat16)


def join(raw, tail):
    vmem = pl.BlockSpec(memory_space=pltpu.VMEM)
    return pl.pallas_call(
        join_kernel,
        out_shape=jax.ShapeDtypeStruct((BLOCK, WIDTH), jnp.bfloat16),
        in_specs=[vmem] * 2,
        out_specs=vmem,
        compiler_params=pltpu.CompilerParams(vmem_limit_bytes=16 << 20),
        name="join",
    )(raw, tail)


def score_kernel(step, given, *refs):
    direct, joined, strips = STEPS[step]
    results = targets(step)
    first = step == "early"
    laid = PAIR if step == "late" else PACKED
    refs = list(refs)

    def take(count):
        taken, refs[:count] = refs[:count], []
        return taken

    in_place = dict(zip(direct, take(len(direct))))
    sources = take(len(joined))
    packed, packed_ids = (None, None) if first else take(2)
    earlier = dict(zip(given, take(len(given))))
    outs = dict(zip(results, take(len(results))))
    if joined:
        held, ids = take(2)
        (sems,) = take(1)
        copies = []
        for i, block in enumerate(sources):
            copies.append(pltpu.make_async_copy(block.at[ROWS:], ids.at[i], sems.at[0, i]))
            copies.append(pltpu.make_async_copy(block.at[:ROWS], held.at[pl.ds(i * ROWS, ROWS)], sems.at[1, i]))
        for copy in copies:
            copy.start()
        for copy in copies:
            copy.wait()

    moves = []
    if step == "second":
        pair, pair_ids = take(2)
        (sems,) = take(1)
        for i, b in enumerate(PAIR):
            at = PACKED.index(b) if b in PACKED else None
            rows = in_place[b].at[:ROWS] if at is None else packed.at[at * ROWS : (at + 1) * ROWS]
            tail = in_place[b].at[ROWS:] if at is None else packed_ids.at[at]
            moves.append(pltpu.make_async_copy(rows, pair.at[i * ROWS : (i + 1) * ROWS], sems.at[0, i]))
            moves.append(pltpu.make_async_copy(tail, pair_ids.at[i], sems.at[1, i]))
        for move in moves:
            move.start()

    def rows_of(blocks):
        b, n = blocks[0], len(blocks)
        if b in in_place:
            return in_place[b][:ROWS, :]
        order, ref = (joined, held) if b in joined else (laid, packed)
        at = order.index(b)
        assert order[at : at + n] == tuple(blocks)
        return ref[at * ROWS : (at + n) * ROWS, :]

    def word(b):
        if b in in_place:
            parts = in_place[b][ROWS:, :ROWS]
        elif b in joined:
            parts = ids[joined.index(b), :, :ROWS]
        else:
            parts = packed_ids[laid.index(b), :, :ROWS]
        parts = parts.astype(jnp.float32)
        return parts[0:1] * 65536.0 + parts[1:2] * 256.0 + parts[2:3]

    over_lanes, over_rows = {}, {}

    def update(table, b, value):
        table[b] = jnp.maximum(table[b], value) if b in table else value

    for a, others, sides in strips:
        scores = lax.dot_general(
            rows_of((a,)), rows_of(others), (((1,), (1,)), ((), ())), preferred_element_type=jnp.float32
        )
        near = jnp.broadcast_to(word(a), (128, ROWS)).T.astype(jnp.int32)
        for i, b in enumerate(others):
            far = word(b).astype(jnp.int32)
            down = []
            for k in range(ROWS // 128):
                at = i * ROWS + k * 128
                mixed = near ^ far[:, k * 128 : (k + 1) * 128]
                partner = (mixed > 0) & (mixed < 65536)
                kept = jnp.where(partner, scores[:, at : at + 128], -1.0)
                if a in sides:
                    update(over_lanes, a, kept)
                down.append(jnp.max(kept.reshape(ROWS // 8, 8, 128), axis=0))
            if b in sides and b != a:
                update(over_rows, b, jnp.concatenate(down, axis=1))

    for b in results:
        value = jnp.full((1, ROWS), -1.0, jnp.float32)
        if b in over_lanes:
            value = jnp.maximum(value, jnp.max(over_lanes[b].T, axis=0, keepdims=True))
        if b in over_rows:
            value = jnp.maximum(value, jnp.max(over_rows[b], axis=0, keepdims=True))
        if b in earlier:
            value = jnp.maximum(value, earlier[b][...])
        outs[b][...] = value
    for move in moves:
        move.wait()


def score(step, blocks, earlier, packed=()):
    direct, joined, strips = STEPS[step]
    results = targets(step)
    given = tuple(b for b in results if b in earlier)
    n = len(PAIR) if step == "second" else len(joined)
    hands_on = step in ("early", "second")
    pairs = sum(len(others) for _, others, _ in strips)
    vmem, free = pl.BlockSpec(memory_space=pltpu.VMEM), pl.BlockSpec(memory_space=pl.ANY)
    shapes = [((n * ROWS, WIDTH), jnp.bfloat16), ((n, TAIL, WIDTH), jnp.bfloat16)] if n else []
    values = pl.pallas_call(
        functools.partial(score_kernel, step, given),
        out_shape=[jax.ShapeDtypeStruct((1, ROWS), jnp.float32)] * len(results)
        + [jax.ShapeDtypeStruct(*shape) for shape in shapes if hands_on],
        in_specs=[vmem] * len(direct) + [free] * len(joined) + [vmem] * (len(packed) + len(given)),
        out_specs=[vmem] * (len(results) + (len(shapes) if hands_on else 0)),
        scratch_shapes=[pltpu.VMEM(*shape) for shape in shapes if not hands_on]
        + ([pltpu.SemaphoreType.DMA((2, n))] if n else []),
        compiler_params=pltpu.CompilerParams(vmem_limit_bytes=28 << 20),
        cost_estimate=pl.CostEstimate(
            flops=2 * pairs * ROWS * ROWS * WIDTH, bytes_accessed=2 * pairs * ROWS * WIDTH, transcendentals=0
        ),
        name="score_" + step,
    )(*[blocks[b] for b in direct + joined], *packed, *[earlier[b] for b in given])
    return {**earlier, **dict(zip(results, values))}, values[len(results) :]


def local(embeddings, cluster_id, source_id):
    whole, tail = prepare(embeddings, cluster_id, source_id)
    blocks = {0: whole}
    for block, by in FIRST:
        if block == 1:
            blocks[block] = join(receive(embeddings, by), receive(tail, by))
        else:
            blocks[block] = receive(whole, by)
    for block, parent, by in SECOND:
        whole = blocks[parent]
        if block in (6, 7):
            whole, _ = lax.optimization_barrier((whole, blocks[4]))
        blocks[block] = receive(whole, by)
    best, packed = score("early", blocks, {})
    best, _ = score("middle", blocks, best, packed)
    best, pair = score("second", blocks, best, packed)
    got = [receive(best[b], OFFSETS[b], back=True) for b in (2, 3)]
    best, _ = score("late", blocks, best, pair)
    got += [receive(best[b], OFFSETS[b], back=True) for b in (8, 4)]
    best, _ = score("last", blocks, best, packed)
    own = best[0]
    for value in got:
        own = jnp.maximum(own, value)
    return own.reshape(ROWS)


def solution(mesh):
    return jax.shard_map(
        local,
        mesh=mesh,
        in_specs=(P(("grp", "blk"), None), P(("grp", "blk")), P(("grp", "blk"))),
        out_specs=P(("grp", "blk")),
        check_vma=False,
    )
```

```python
import functools

import jax
import jax.numpy as jnp
from jax import lax
from jax.experimental import pallas as pl
from jax.experimental.pallas import tpu as pltpu
from jax.sharding import PartitionSpec as P

TORUS = (2, 4, 4)
OFFSETS = (
    (0, 0, 0),
    (0, 0, 3),
    (0, 1, 0),
    (0, 3, 1),
    (1, 0, 0),
    (0, 0, 2),
    (0, 2, 0),
    (0, 2, 2),
    (1, 0, 3),
)
FIRST = ((1, (0, 0, 3)), (2, (0, 1, 0)), (3, (0, 3, 1)), (4, (1, 0, 0)))
SECOND = ((8, 1, (1, 0, 0)), (5, 1, (0, 0, 3)), (6, 2, (0, 1, 0)), (7, 3, (0, 3, 1)))
ROWS = 384
TAIL = 16
BLOCK = ROWS + TAIL
WIDTH = 1024
STRIPE = 192
STRIPES = ROWS // STRIPE
PACKED = (1, 0, 2, 3, 4)
PAIR = (8, 4)
STEPS = {
    "early": (
        (),
        PACKED,
        ((0, PACKED, (0, 2, 3)), (1, (2, 3, 4), (2, 3, 4)), (2, (3, 4), (2, 3, 4)), (3, (4,), (3, 4))),
    ),
    "middle": ((5,), (), ((5, (2, 3, 4), (2, 3, 4)),)),
    "second": ((8,), (), ((8, (0, 2, 3, 4), (2, 3, 8)),)),
    "late": ((6, 7), (), ((7, PAIR, PAIR), (6, PAIR, PAIR))),
    "last": ((), (5, 7, 6), ((0, (5, 7, 6), (0,)),)),
}


def difference(a, b):
    return tuple((p - q) % n for p, q, n in zip(a, b, TORUS))


def targets(step):
    return tuple(sorted({b for a, others, sides in STEPS[step][2] for b in sides if b in (a, *others)}))


def check():
    met = set()
    for _, _, strips in STEPS.values():
        for a, others, sides in strips:
            for b in others:
                met |= {difference(OFFSETS[b], OFFSETS[a])} if a in sides else set()
                met |= {difference(OFFSETS[a], OFFSETS[b])} if b in sides else set()
    assert len(met) == 32
    assert all(OFFSETS[block] == by for block, by in FIRST)
    assert all(difference(OFFSETS[block], OFFSETS[parent]) == by for block, parent, by in SECOND)


check()


def flat(y, z, x):
    return ((y % TORUS[0]) * TORUS[1] + z % TORUS[1]) * TORUS[2] + x % TORUS[2]


def receive(array, by, back=False):
    links = []
    for y in range(TORUS[0]):
        for z in range(TORUS[1]):
            for x in range(TORUS[2]):
                far, near = flat(y + by[0], z + by[1], x + by[2]), flat(y, z, x)
                links.append((near, far) if back else (far, near))
    return lax.ppermute(array, "blk", links)


def unit_rows(rows):
    widened = rows.astype(jnp.float32)
    factor = lax.rsqrt(jnp.mean(widened * widened, axis=1, keepdims=True) + 1e-06) / 32.0
    return (widened * factor).astype(jnp.bfloat16)


def prepare_kernel(embeddings, cluster, source, out, out_tail, raw, clusters, sources, unit, short, sems):
    def copy(source_rows, target_rows, sem):
        return pltpu.make_async_copy(source_rows, target_rows, sems.at[sem])

    stripes = [slice(i * STRIPE, (i + 1) * STRIPE) for i in range(STRIPES)]
    ids = [copy(cluster, clusters, 2 * STRIPES), copy(source, sources, 2 * STRIPES + 1)]
    arriving = [copy(embeddings.at[rows], raw.at[rows], i) for i, rows in enumerate(stripes)]
    leaving = [copy(unit.at[rows], out.at[rows], STRIPES + i) for i, rows in enumerate(stripes)]
    leaving.append(copy(unit.at[ROWS:], out.at[ROWS:], 2 * STRIPES + 2))
    leaving.append(copy(short, out_tail, 2 * STRIPES + 3))
    for move in ids + arriving:
        move.start()
    for move in ids:
        move.wait()
    line = lax.broadcasted_iota(jnp.int32, (TAIL, ROWS), 0)
    number = sources[...].reshape(1, ROWS)
    rank = clusters[...].reshape(1, ROWS)
    tail = jnp.where(line == 0, rank, jnp.where(line == 1, number // 256, jnp.where(line == 2, number % 256, 0)))
    tail = tail.astype(jnp.float32)
    unit[ROWS:, :ROWS] = tail.astype(jnp.bfloat16)
    pieces = [tail[i : i + 1, k * 128 : (k + 1) * 128] for i in range(3) for k in range(ROWS // 128)]
    pieces.append(jnp.zeros((TAIL - len(pieces), 128), jnp.float32))
    short[...] = jnp.concatenate(pieces, axis=0).astype(jnp.bfloat16)
    unit[ROWS:, ROWS:] = jnp.zeros((TAIL, WIDTH - ROWS), jnp.bfloat16)
    leaving[STRIPES].start()
    leaving[STRIPES + 1].start()
    for i, rows in enumerate(stripes):
        arriving[i].wait()
        unit[rows, :] = unit_rows(raw[rows, :])
        leaving[i].start()
    for move in leaving:
        move.wait()


def prepare(embeddings, cluster_id, source_id):
    far = pl.BlockSpec(memory_space=pltpu.HBM)
    return pl.pallas_call(
        prepare_kernel,
        out_shape=[jax.ShapeDtypeStruct(shape, jnp.bfloat16) for shape in ((BLOCK, WIDTH), (TAIL, 128))],
        in_specs=[far] * 3,
        out_specs=[far] * 2,
        scratch_shapes=[
            pltpu.VMEM((ROWS, WIDTH), jnp.bfloat16),
            pltpu.VMEM((ROWS,), jnp.int32),
            pltpu.VMEM((ROWS,), jnp.int32),
            pltpu.VMEM((BLOCK, WIDTH), jnp.bfloat16),
            pltpu.VMEM((TAIL, 128), jnp.bfloat16),
            pltpu.SemaphoreType.DMA((2 * STRIPES + 4,)),
        ],
        compiler_params=pltpu.CompilerParams(vmem_limit_bytes=60 << 20),
        name="prepare",
    )(embeddings, cluster_id, source_id)


def join_kernel(raw, tail, out):
    for i in range(STRIPES):
        rows = slice(i * STRIPE, (i + 1) * STRIPE)
        out[rows, :] = unit_rows(raw[rows, :])
    short = tail[...].astype(jnp.float32)
    n = ROWS // 128
    lines = [jnp.concatenate([short[i * n + k : i * n + k + 1] for k in range(n)], axis=1) for i in range(3)]
    lines.append(jnp.zeros((TAIL - 3, ROWS), jnp.float32))
    out[ROWS:, :ROWS] = jnp.concatenate(lines, axis=0).astype(jnp.bfloat16)
    out[ROWS:, ROWS:] = jnp.zeros((TAIL, WIDTH - ROWS), jnp.bfloat16)


def join(raw, tail):
    vmem = pl.BlockSpec(memory_space=pltpu.VMEM)
    return pl.pallas_call(
        join_kernel,
        out_shape=jax.ShapeDtypeStruct((BLOCK, WIDTH), jnp.bfloat16),
        in_specs=[vmem] * 2,
        out_specs=vmem,
        compiler_params=pltpu.CompilerParams(vmem_limit_bytes=16 << 20),
        name="join",
    )(raw, tail)


def score_kernel(step, given, *refs):
    direct, joined, strips = STEPS[step]
    results = targets(step)
    first = step == "early"
    laid = PAIR if step == "late" else PACKED
    refs = list(refs)

    def take(count):
        taken, refs[:count] = refs[:count], []
        return taken

    in_place = dict(zip(direct, take(len(direct))))
    sources = take(len(joined))
    packed, packed_ids = (None, None) if first else take(2)
    earlier = dict(zip(given, take(len(given))))
    outs = dict(zip(results, take(len(results))))
    if joined:
        held, ids = take(2)
        (sems,) = take(1)
        copies = []
        for i, block in enumerate(sources):
            copies.append(pltpu.make_async_copy(block.at[ROWS:], ids.at[i], sems.at[0, i]))
            copies.append(pltpu.make_async_copy(block.at[:ROWS], held.at[pl.ds(i * ROWS, ROWS)], sems.at[1, i]))
        for copy in copies:
            copy.start()
        for copy in copies:
            copy.wait()

    moves = []
    if step == "second":
        pair, pair_ids = take(2)
        (sems,) = take(1)
        for i, b in enumerate(PAIR):
            at = PACKED.index(b) if b in PACKED else None
            rows = in_place[b].at[:ROWS] if at is None else packed.at[at * ROWS : (at + 1) * ROWS]
            tail = in_place[b].at[ROWS:] if at is None else packed_ids.at[at]
            moves.append(pltpu.make_async_copy(rows, pair.at[i * ROWS : (i + 1) * ROWS], sems.at[0, i]))
            moves.append(pltpu.make_async_copy(tail, pair_ids.at[i], sems.at[1, i]))
        for move in moves:
            move.start()

    def rows_of(blocks):
        b, n = blocks[0], len(blocks)
        if b in in_place:
            return in_place[b][:ROWS, :]
        order, ref = (joined, held) if b in joined else (laid, packed)
        at = order.index(b)
        assert order[at : at + n] == tuple(blocks)
        return ref[at * ROWS : (at + n) * ROWS, :]

    def word(b):
        if b in in_place:
            parts = in_place[b][ROWS:, :ROWS]
        elif b in joined:
            parts = ids[joined.index(b), :, :ROWS]
        else:
            parts = packed_ids[laid.index(b), :, :ROWS]
        parts = parts.astype(jnp.float32)
        return parts[0:1] * 65536.0 + parts[1:2] * 256.0 + parts[2:3]

    over_lanes, over_rows = {}, {}

    def update(table, b, value):
        table[b] = jnp.maximum(table[b], value) if b in table else value

    for a, others, sides in strips:
        scores = lax.dot_general(
            rows_of((a,)), rows_of(others), (((1,), (1,)), ((), ())), preferred_element_type=jnp.float32
        )
        near = jnp.broadcast_to(word(a), (128, ROWS)).T.astype(jnp.int32)
        for i, b in enumerate(others):
            far = word(b).astype(jnp.int32)
            down = []
            for k in range(ROWS // 128):
                at = i * ROWS + k * 128
                mixed = near ^ far[:, k * 128 : (k + 1) * 128]
                partner = (mixed > 0) & (mixed < 65536)
                kept = jnp.where(partner, scores[:, at : at + 128], -1.0)
                if a in sides:
                    update(over_lanes, a, kept)
                down.append(jnp.max(kept.reshape(ROWS // 8, 8, 128), axis=0))
            if b in sides and b != a:
                update(over_rows, b, jnp.concatenate(down, axis=1))

    for b in results:
        value = jnp.full((1, ROWS), -1.0, jnp.float32)
        if b in over_lanes:
            value = jnp.maximum(value, jnp.max(over_lanes[b].T, axis=0, keepdims=True))
        if b in over_rows:
            value = jnp.maximum(value, jnp.max(over_rows[b], axis=0, keepdims=True))
        if b in earlier:
            value = jnp.maximum(value, earlier[b][...])
        outs[b][...] = value
    for move in moves:
        move.wait()


def score(step, blocks, earlier, packed=()):
    direct, joined, strips = STEPS[step]
    results = targets(step)
    given = tuple(b for b in results if b in earlier)
    n = len(PAIR) if step == "second" else len(joined)
    hands_on = step in ("early", "second")
    pairs = sum(len(others) for _, others, _ in strips)
    vmem, free = pl.BlockSpec(memory_space=pltpu.VMEM), pl.BlockSpec(memory_space=pl.ANY)
    shapes = [((n * ROWS, WIDTH), jnp.bfloat16), ((n, TAIL, WIDTH), jnp.bfloat16)] if n else []
    values = pl.pallas_call(
        functools.partial(score_kernel, step, given),
        out_shape=[jax.ShapeDtypeStruct((1, ROWS), jnp.float32)] * len(results)
        + [jax.ShapeDtypeStruct(*shape) for shape in shapes if hands_on],
        in_specs=[vmem] * len(direct) + [free] * len(joined) + [vmem] * (len(packed) + len(given)),
        out_specs=[vmem] * (len(results) + (len(shapes) if hands_on else 0)),
        scratch_shapes=[pltpu.VMEM(*shape) for shape in shapes if not hands_on]
        + ([pltpu.SemaphoreType.DMA((2, n))] if n else []),
        compiler_params=pltpu.CompilerParams(vmem_limit_bytes=28 << 20),
        cost_estimate=pl.CostEstimate(
            flops=2 * pairs * ROWS * ROWS * WIDTH, bytes_accessed=2 * pairs * ROWS * WIDTH, transcendentals=0
        ),
        name="score_" + step,
    )(*[blocks[b] for b in direct + joined], *packed, *[earlier[b] for b in given])
    return {**earlier, **dict(zip(results, values))}, values[len(results) :]


def local(embeddings, cluster_id, source_id):
    whole, tail = prepare(embeddings, cluster_id, source_id)
    blocks = {0: whole}
    for block, by in FIRST:
        if block == 1:
            blocks[block] = join(receive(embeddings, by), receive(tail, by))
        else:
            blocks[block] = receive(whole, by)
    for block, parent, by in SECOND:
        whole = blocks[parent]
        if block in (6, 7):
            whole, _ = lax.optimization_barrier((whole, blocks[4]))
        blocks[block] = receive(whole, by)
    best, packed = score("early", blocks, {})
    best, _ = score("middle", blocks, best, packed)
    best, pair = score("second", blocks, best, packed)
    got = [receive(best[b], OFFSETS[b], back=True) for b in (2, 3)]
    best, _ = score("late", blocks, best, pair)
    got += [receive(best[b], OFFSETS[b], back=True) for b in (4, 8)]
    best, _ = score("last", blocks, best, packed)
    own = best[0]
    for value in got:
        own = jnp.maximum(own, value)
    return own.reshape(ROWS)


def solution(mesh):
    return jax.shard_map(
        local,
        mesh=mesh,
        in_specs=(P(("grp", "blk"), None), P(("grp", "blk")), P(("grp", "blk"))),
        out_specs=P(("grp", "blk")),
        check_vma=False,
    )
```
